256 devices in a mesh: vp: 64 (over x, z, core), red: 4 (over y).
Axes of the slice: x: 4, y: 4, z: 8, core: 2. Of those that a mesh axis runs over, the one named last changes fastest.
Arguments:
- virt_sizes: int32 [8], replicated, may hold values from 1 to 320, as said below
- occ_sizes: int32 [8], replicated, may hold values from 1 to 40, as said below
- pair_ids: int32 [1536], replicated, may hold values from 0 to 39999
- amplitudes: bfloat16 [1536, 6400], P('vp', 'red'), may hold values from -6 to 6
- integrals: bfloat16 [102400, 6400], P('vp', 'red'), may hold values from -0.21875 to 0.21875
Outputs:
- ladder: bfloat16 [1536, 102400], P('red', 'vp')
The draws below stay inside these ranges and needn't reach their ends.
Inputs may be any that keep to these rules, and one draw needn't show every extreme that they name: `virt_sizes`: each entry lies in 1..320, the entries sum to 1600, and one entry equals 320. `occ_sizes`: each entry lies in 1..40, the entries sum to 200, and one entry equals 40.
All inputs are finite; a program needn't handle non-finite values.
Results may differ from the reference program's by a relative error of at most 0.013.
Values may be sent and summed in bfloat16 or wider, within the bound.
No kernel may reach another device: no remote copies, remote signals or barrier semaphores. Data moves between devices by JAX's collectives and lax.ppermute only.
A program may use at most 64 MiB of HBM per device.

```python
import jax
import jax.numpy as jnp
from jax import lax

VIRT = 1600
NOCC = 200
PAIRS = 1536
BMAX = 320
OMAX = 40
ROWORB = 64
COLORB = 4
N_VP = 64
N_RED = 4


def block_sizes(key, total, largest):
    first, second = jax.random.split(key)
    weights = jax.random.randint(first, (7,), 4, 7)
    remain = total - largest - 7
    base = 1 + remain * weights // jnp.sum(weights)
    short = total - largest - jnp.sum(base)
    base = base + (jnp.arange(7) < short).astype(jnp.int32)
    sizes = jnp.concatenate([jnp.array([largest], jnp.int32), base.astype(jnp.int32)])
    return jnp.roll(sizes, jax.random.randint(second, (), 0, 8)).astype(jnp.int32)


def draw_virt_sizes(key, part):
    key = jax.random.fold_in(key, 11)
    return block_sizes(key, VIRT, BMAX)


def draw_occ_sizes(key, part):
    key = jax.random.fold_in(key, 23)
    return block_sizes(key, NOCC, OMAX)


def with_ends(drawn, stream_key, least, high):
    place = [jax.random.randint(jax.random.fold_in(stream_key, axis), (), 0, length) for axis, length in enumerate(drawn.shape)]
    longest = drawn.shape.index(max(drawn.shape))
    beside = place[:longest] + [(place[longest] + 1) % drawn.shape[longest]] + place[longest + 1:]
    return drawn.at[tuple(place)].set(least).at[tuple(beside)].set(high)


def block_levels(key, shape, shards, smallest, top_value):
    def one(position, blocks):
        draws = jax.random.uniform(jax.random.fold_in(jax.random.fold_in(key, 6), position), (blocks,), jnp.float32, smallest / len(shards), top_value / len(shards))
        return jnp.repeat(jnp.exp(draws), shape[position] // blocks).reshape((-1,) + (1,) * (len(shape) - position - 1))

    level = one(*shards[0])
    for cut in shards[1:]:
        level = level * one(*cut)
    return level


def centred(rng, extent, width, reach, pieces=(), kind=jnp.bfloat16):
    drawn = jax.random.normal(rng, extent, jnp.float32) * width
    if len(pieces) > 0:
        drawn = block_levels(rng, extent, pieces, -0.22, 0.18) * drawn
    return jnp.clip(drawn, min=-reach, max=reach).astype(kind)


def setup_inputs(seed: int = 0) -> dict:
    splits = jax.random.split(jax.random.key(seed), 6)
    return {
        "virt_sizes": draw_virt_sizes(jax.random.fold_in(splits[5], 71), 0),
        "occ_sizes": draw_occ_sizes(jax.random.fold_in(splits[5], 71), 0),
        "pair_ids": with_ends(jax.random.randint(splits[2], (PAIRS,), 0, NOCC * NOCC), jax.random.fold_in(splits[2], 1), 0, (NOCC * NOCC) - 1).astype(jnp.int32),
        "amplitudes": centred(splits[3], (PAIRS, COLORB * VIRT), 1.0, 6.0, ((0, 64), (1, 4))),
        "integrals": centred(splits[4], (ROWORB * VIRT, COLORB * VIRT), (VIRT // 2) ** -0.5, 0.21875, ((0, 64), (1, 4))),
    }


def irrep_of(positions, sizes):
    bounds = jnp.cumsum(sizes)[:7]
    return jnp.sum((positions[:, None] >= bounds[None, :]).astype(jnp.int32), axis=1)


def reference(virt_sizes, occ_sizes, pair_ids, amplitudes, integrals):
    orbital = irrep_of(jnp.arange(VIRT, dtype=jnp.int32), virt_sizes)
    row_irrep = irrep_of(jnp.arange(N_VP, dtype=jnp.int32) * (VIRT // N_VP), virt_sizes)
    col_irrep = irrep_of(jnp.arange(N_RED, dtype=jnp.int32) * (VIRT // N_RED), virt_sizes)
    first = irrep_of(pair_ids // NOCC, occ_sizes)
    second = irrep_of(pair_ids % NOCC, occ_sizes)
    occ_pair = jnp.bitwise_xor(first, second)

    def one_row(index):
        rows = lax.dynamic_slice_in_dim(integrals, index * VIRT, VIRT, 0)
        row_pair = jnp.bitwise_xor(jnp.sum(jnp.where(jnp.arange(N_VP) == index, row_irrep, 0)), orbital)
        total = jnp.zeros((PAIRS, VIRT), jnp.float32)
        for column in range(N_RED):
            block = rows[:, column * VIRT:(column + 1) * VIRT]
            col_pair = jnp.bitwise_xor(col_irrep[column], orbital)
            masked = jnp.where(row_pair[:, None] == col_pair[None, :], block, jnp.zeros_like(block))
            slab = amplitudes[:, column * VIRT:(column + 1) * VIRT]
            term = lax.dot_general(slab, masked, (((1,), (1,)), ((), ())), preferred_element_type=jnp.float32)
            total = total + term.astype(jnp.bfloat16).astype(jnp.float32)
        keep = jnp.bitwise_xor(occ_pair[:, None], row_pair[None, :]) == 0
        return jnp.where(keep, total, jnp.zeros_like(total)).astype(jnp.bfloat16)

    stacked = lax.map(one_row, jnp.arange(N_VP, dtype=jnp.int32))
    return jnp.transpose(stacked, (1, 0, 2)).reshape(PAIRS, N_VP * VIRT)
```

```python
import functools

import jax
import jax.numpy as jnp
from jax import lax
from jax.experimental import pallas as pl
from jax.experimental.pallas import tpu as pltpu
from jax.sharding import Mesh, PartitionSpec as P

VIRT = 1600
NOCC = 200
PAIRS = 1536
BMAX = 320
NX, NZ, NC, NY = 4, 8, 2, 4
AWIDTH = VIRT // (NX * NZ * NC)
CWIDTH = VIRT // NY
ROWS = PAIRS // (NX * NZ * NC)
HALF = NZ * ROWS
PORTION = NC * HALF
LANES = 384
MAIN = 256
WINDOW = 336
SPAN = 512
LAST = 1152
F32, BF16, I32 = jnp.float32, jnp.bfloat16, jnp.int32
SMEM = pl.BlockSpec(memory_space=pltpu.SMEM)
VMEM = pl.BlockSpec(memory_space=pltpu.VMEM)


def offset_of(sizes_ref, group):
    total = jnp.int32(0)
    for g in range(7):
        total += jnp.where(group > g, sizes_ref[g], 0)
    return total


def irrep_of(position, sizes_ref):
    bound, irrep = jnp.int32(0), jnp.zeros_like(position)
    for g in range(7):
        bound += sizes_ref[g]
        irrep += (position >= bound).astype(I32)
    return irrep


def pair_sym(ids, sizes_ref):
    first = lax.shift_right_logical(ids * 5243, 20)
    second = ids - first * NOCC
    return jnp.bitwise_xor(irrep_of(first, sizes_ref), irrep_of(second, sizes_ref))


def vp_index():
    return (lax.axis_index("x") * NZ + lax.axis_index("z")) * NC + lax.axis_index("c")


def row_irrep(virt_ref):
    return irrep_of(vp_index() * AWIDTH, virt_ref)


def col_irrep(virt_ref):
    return irrep_of(lax.axis_index("y") * CWIDTH, virt_ref)


def block_start(offset):
    return jnp.minimum(lax.div(offset, 16) * 16, VIRT - WINDOW)


def load_span(source_ref, span_ref, rows, offset):
    @pl.when(offset < LAST)
    def _():
        start = pl.multiple_of(lax.div(offset, 128) * 128, 128)
        span_ref[...] = source_ref[rows, pl.ds(start, SPAN)]

    @pl.when(offset >= LAST)
    def _():
        span_ref[:, :384] = source_ref[rows, LAST:1536]
        span_ref[:, 384:448] = source_ref[rows, 1536:1600]
        span_ref[:, 448:] = jnp.zeros((span_ref.shape[0], 64), span_ref.dtype)

    shift = jnp.where(offset < LAST, lax.rem(offset, 128), offset - LAST)
    return lax.rem(SPAN - shift, SPAN)


def pack_kernel(virt_ref, occ_ref, ids_ref, t_ref, out_ref, wide, span):
    wide[...] = t_ref[...].astype(F32)
    hc = col_irrep(virt_ref)
    base = vp_index() * ROWS
    row = lax.broadcasted_iota(I32, (ROWS, LANES), 0)
    lane = lax.broadcasted_iota(I32, (ROWS, LANES), 1)
    sym = jnp.zeros((ROWS, LANES), I32)
    for r in range(ROWS):
        sym = jnp.where(row == r, pair_sym(ids_ref[base + r], occ_ref), sym)
    packed = jnp.where(lane >= BMAX, sym.astype(F32), 0.0)
    for s in range(8):
        group = jnp.bitwise_xor(hc, s)
        turn = load_span(wide, span, slice(None), offset_of(virt_ref, group))
        block = pltpu.roll(span[...], turn, 1)[:, :LANES]
        packed = jnp.where((sym == s) & (lane < virt_ref[group]), block, packed)
    out_ref[...] = jnp.concatenate([packed] * NZ, axis=0).astype(BF16)


def blocks_kernel(virt_ref, occ_ref, ids_ref, v_ref, after_ref, out_ref, order_ref, sym_ref, span):
    del after_ref
    ra, hc = row_irrep(virt_ref), col_irrep(virt_ref)
    lane = lax.broadcasted_iota(I32, (WINDOW, LANES), 1)
    for s in range(8):
        group = jnp.bitwise_xor(hc, s)
        start = block_start(offset_of(virt_ref, jnp.bitwise_xor(ra, s)))
        rows = pl.ds(pl.multiple_of(start, 16), WINDOW)
        turn = load_span(v_ref, span, rows, offset_of(virt_ref, group))
        block = pltpu.roll(span[...].astype(F32), turn, 1)[:, :LANES]
        block = jnp.where(lane < virt_ref[group], block, 0.0).astype(BF16)
        out_ref[:, s * MAIN:(s + 1) * MAIN] = block[:, :MAIN]
        out_ref[:, 8 * MAIN + s * 128:8 * MAIN + (s + 1) * 128] = block[:, MAIN:]
    column = lax.broadcasted_iota(I32, (PORTION, PORTION), 0)
    target = lax.broadcasted_iota(I32, (PORTION, PORTION), 1)
    other = (column >= HALF).astype(I32)
    within = column - other * HALF
    z = lax.shift_right_logical(within * 2731, 16)
    core = jnp.bitwise_xor(lax.axis_index("c"), other)
    order_ref[...] = ((z * NC + core) * ROWS + (within - z * ROWS) == target).astype(F32).astype(BF16)
    ids = ids_ref[pl.ds(lax.axis_index("y"), 1), :]
    sym_ref[...] = jnp.broadcast_to(pair_sym(ids, occ_ref), (8, PORTION))


def terms_kernel(virt_ref, own_ref, other_ref, v_ref, o0, o1, o2, o3, stack, total):
    hc = col_irrep(virt_ref)
    x, y = lax.axis_index("x"), lax.axis_index("y")
    for r, out_ref in ((2, o2), (1, o1), (3, o3), (0, o0)):
        portion = lax.rem(y + r, NY)
        rows = pl.ds(pl.multiple_of(lax.rem(x - portion + NX, NX) * HALF, HALF), HALF)
        t = jnp.concatenate([own_ref[rows, :], other_ref[rows, :]], axis=0)
        sym = jnp.broadcast_to(t[:, BMAX:BMAX + 1].astype(F32), (PORTION, MAIN))
        for s in range(8):
            keep = (sym == s).astype(F32).astype(BF16)
            stack[:, s * MAIN:(s + 1) * MAIN] = t[:, :MAIN] * keep
        nt = (((1,), (1,)), ((), ()))
        total[...] = lax.dot_general(v_ref[:, :8 * MAIN], stack[...], nt, preferred_element_type=F32)
        for s in range(8):

            @pl.when(virt_ref[jnp.bitwise_xor(hc, s)] > MAIN)
            def _():
                keep = (sym[:, :128] == s).astype(F32).astype(BF16)
                total[...] += lax.dot_general(
                    v_ref[:, 8 * MAIN + s * 128:8 * MAIN + (s + 1) * 128], t[:, MAIN:] * keep, nt,
                    preferred_element_type=F32)

        out_ref[...] = total[...].astype(BF16)


def place_kernel(virt_ref, a_ref, b_ref, c_ref, d_ref, order_ref, sym_ref, out_ref):
    ra = row_irrep(virt_ref)
    total = a_ref[...].astype(F32) + b_ref[...].astype(F32) + c_ref[...].astype(F32) + d_ref[...].astype(F32)
    total = jnp.dot(total.astype(BF16), order_ref[...], preferred_element_type=F32)
    out_ref[...] = jnp.zeros_like(out_ref)
    row = lax.broadcasted_iota(I32, (WINDOW, PORTION), 0)
    sym = jnp.broadcast_to(sym_ref[:1, :], (WINDOW, PORTION))
    for s in range(8):
        group = jnp.bitwise_xor(ra, s)
        offset = offset_of(virt_ref, group)
        start = block_start(offset)
        rows = pl.ds(pl.multiple_of(start, 16), WINDOW)
        first = offset - start
        keep = (row >= first) & (row < first + virt_ref[group])
        value = jnp.where(sym == s, total, 0.0)
        out_ref[rows, :] = jnp.where(keep, value, out_ref[rows, :].astype(F32)).astype(BF16)


def shift(value, axis, size, by):
    return lax.ppermute(value, axis, [(i, (i + by) % size) for i in range(size)])


def call(kernel, specs, out, scratch=(), flops=0, moved=0):
    return pl.pallas_call(
        kernel,
        in_specs=specs,
        out_specs=jax.tree.map(lambda _: VMEM, out),
        out_shape=out,
        scratch_shapes=list(scratch),
        compiler_params=pltpu.CompilerParams(vmem_limit_bytes=48 * 2**20),
        cost_estimate=pl.CostEstimate(flops=flops, bytes_accessed=moved, transcendentals=0),
    )


def shards(virt_sizes, occ_sizes, pair_ids, amplitudes, integrals):
    shape = jax.ShapeDtypeStruct
    packed = call(
        pack_kernel, [SMEM, SMEM, SMEM, VMEM], shape((HALF, LANES), BF16),
        [pltpu.VMEM((ROWS, VIRT), F32), pltpu.VMEM((ROWS, SPAN), F32)], moved=300000,
    )(virt_sizes, occ_sizes, pair_ids, amplitudes)
    mine = lax.all_to_all(packed, "z", 0, 0, tiled=True)
    across = [shift(mine, "x", NX, k) for k in (2, 1, 3)]
    blocks, order, sym = call(
        blocks_kernel, [SMEM, SMEM, VMEM, VMEM, VMEM],
        (shape((WINDOW, 8 * LANES), BF16), shape((PORTION, PORTION), BF16), shape((8, PORTION), I32)),
        [pltpu.VMEM((WINDOW, SPAN), BF16)], moved=12000000,
    )(virt_sizes, occ_sizes, pair_ids.reshape(NY, PORTION), integrals, mine[:16, :128])
    own = jnp.concatenate([mine, across[1], across[0], across[2]], axis=0)
    other = shift(own, "c", NC, 1)
    tile = shape((WINDOW, PORTION), BF16)
    terms = call(
        terms_kernel, [SMEM, VMEM, VMEM, VMEM], (tile,) * NY,
        [pltpu.VMEM((PORTION, 8 * MAIN), BF16), pltpu.VMEM((WINDOW, PORTION), F32)],
        flops=2 * PAIRS * WINDOW * 8 * MAIN, moved=4500000,
    )(virt_sizes, own, other, blocks)
    far = [shift(terms[r], "y", NY, r) for r in (2, 1, 3)]
    out = call(
        place_kernel, [SMEM] + [VMEM] * 6, shape((VIRT, PORTION), BF16), moved=2600000,
    )(virt_sizes, terms[0], *far, order, sym)
    return out.T


def solution(mesh):
    grid = Mesh(mesh.devices.reshape(NX, NZ, NC, NY), ("x", "z", "c", "y"))
    vp = ("x", "z", "c")
    in_specs = (P(), P(), P(), P(vp, "y"), P(vp, "y"))
    return jax.shard_map(shards, mesh=grid, in_specs=in_specs, out_specs=P("y", vp), check_vma=False)
```

```python
import functools

import jax
import jax.numpy as jnp
from jax import lax
from jax.experimental import pallas as pl
from jax.experimental.pallas import tpu as pltpu
from jax.sharding import Mesh, PartitionSpec as P

VIRT = 1600
NOCC = 200
PAIRS = 1536
BMAX = 320
NX, NZ, NC, NY = 4, 8, 2, 4
AWIDTH = VIRT // (NX * NZ * NC)
CWIDTH = VIRT // NY
ROWS = PAIRS // (NX * NZ * NC)
HALF = NZ * ROWS
PORTION = NC * HALF
LANES = 384
MAIN = 256
WINDOW = 352
FOLD = WINDOW // 2
MESSAGE = WINDOW + FOLD
SPAN = 512
LAST = 1152
F32, BF16, I32 = jnp.float32, jnp.bfloat16, jnp.int32
SMEM = pl.BlockSpec(memory_space=pltpu.SMEM)
VMEM = pl.BlockSpec(memory_space=pltpu.VMEM)
HBM = pl.BlockSpec(memory_space=pltpu.HBM)
NT = (((1,), (1,)), ((), ()))


def offset_of(sizes_ref, group):
    total = jnp.int32(0)
    for g in range(7):
        total += jnp.where(group > g, sizes_ref[g], 0)
    return total


def irrep_of(position, sizes_ref):
    bound, irrep = jnp.int32(0), jnp.zeros_like(position)
    for g in range(7):
        bound += sizes_ref[g]
        irrep += (position >= bound).astype(I32)
    return irrep


def pair_sym(ids, sizes_ref):
    first = lax.shift_right_logical(ids * 5243, 20)
    second = ids - first * NOCC
    return jnp.bitwise_xor(irrep_of(first, sizes_ref), irrep_of(second, sizes_ref))


def vp_index():
    return (lax.axis_index("x") * NZ + lax.axis_index("z")) * NC + lax.axis_index("c")


def row_irrep(virt_ref):
    return irrep_of(vp_index() * AWIDTH, virt_ref)


def col_irrep(virt_ref):
    return irrep_of(lax.axis_index("y") * CWIDTH, virt_ref)


def block_start(offset):
    return pl.multiple_of(lax.div(offset, 16) * 16, 16)


def load_span(source_ref, span_ref, offset):
    @pl.when(offset < LAST)
    def _():
        start = pl.multiple_of(lax.div(offset, 128) * 128, 128)
        span_ref[...] = source_ref[:, pl.ds(start, SPAN)]

    @pl.when(offset >= LAST)
    def _():
        span_ref[:, :384] = source_ref[:, LAST:1536]
        span_ref[:, 384:448] = source_ref[:, 1536:1600]
        span_ref[:, 448:] = jnp.zeros((span_ref.shape[0], 64), span_ref.dtype)

    shift = jnp.where(offset < LAST, lax.rem(offset, 128), offset - LAST)
    return lax.rem(SPAN - shift, SPAN)


def pack_kernel(virt_hbm, occ_hbm, ids_hbm, t_hbm, out_ref, virt_out, occ_out,
                virt_ref, occ_ref, ids_ref, t_ref, wide, span, sems):
    pairs = ((virt_hbm, virt_ref), (occ_hbm, occ_ref), (ids_hbm, ids_ref), (t_hbm, t_ref))
    copies = [pltpu.make_async_copy(a, b, sems.at[i]) for i, (a, b) in enumerate(pairs)]
    for copy in copies:
        copy.start()
    for copy in copies:
        copy.wait()
    for g in range(8):
        virt_out[g] = virt_ref[g]
        occ_out[g] = occ_ref[g]
    wide[...] = t_ref[...].astype(F32)
    hc = col_irrep(virt_ref)
    base = vp_index() * ROWS
    row = lax.broadcasted_iota(I32, (ROWS, LANES), 0)
    lane = lax.broadcasted_iota(I32, (ROWS, LANES), 1)
    sym = jnp.zeros((ROWS, LANES), I32)
    for r in range(ROWS):
        sym = jnp.where(row == r, pair_sym(ids_ref[base + r], occ_ref), sym)
    packed = jnp.where(lane >= BMAX, sym.astype(F32), 0.0)
    for s in range(8):
        group = jnp.bitwise_xor(hc, s)
        turn = load_span(wide, span, offset_of(virt_ref, group))
        block = pltpu.roll(span[...], turn, 1)[:, :LANES]
        packed = jnp.where((sym == s) & (lane < virt_ref[group]), block, packed)
    out_ref[...] = jnp.concatenate([packed] * NZ, axis=0).astype(BF16)


def blocks_kernel(virt_ref, occ_ref, ids_ref, v_hbm, mine_ref, out_ref, order_ref, sym_ref, copy_ref,
                  windows, span, rolled, sems):
    ra, hc = row_irrep(virt_ref), col_irrep(virt_ref)
    starts = [block_start(offset_of(virt_ref, jnp.bitwise_xor(ra, s))) for s in range(8)]
    firsts = [pl.multiple_of(jnp.minimum(start, VIRT - WINDOW), 16) for start in starts]
    copies = [
        pltpu.make_async_copy(v_hbm.at[pl.ds(firsts[s], WINDOW), :], windows.at[s], sems.at[s]) for s in range(8)
    ]
    for copy in copies:
        copy.start()
    copy_ref[...] = mine_ref[...]
    rolled[WINDOW:, :] = jnp.zeros((WINDOW, LANES), BF16)
    odd = jnp.bitwise_and(lax.axis_index("x") + lax.axis_index("y"), 1) == 1
    column = lax.broadcasted_iota(I32, (128, PORTION), 0)
    target = lax.broadcasted_iota(I32, (128, PORTION), 1)
    for half in range(2):
        core = jnp.bitwise_xor(lax.axis_index("c"), half)

        def hits(position):
            z = lax.shift_right_logical(position * 2731, 16)
            return (z * NC + core) * ROWS + (position - z * ROWS) == target

        full = hits(column + jnp.where(odd, 64, 0))
        part = hits(jnp.bitwise_and(column, 63) + jnp.where(odd, 0, 128))
        order_ref[half * 128:half * 128 + 128, :] = full.astype(F32).astype(BF16)
        order_ref[256 + half * 128:384 + half * 128, :] = (part & (column < 64)).astype(F32).astype(BF16)
        order_ref[512 + half * 128:640 + half * 128, :] = (part & (column >= 64)).astype(F32).astype(BF16)
    ids = ids_ref[pl.ds(lax.axis_index("y"), 1), :]
    sym_ref[...] = jnp.broadcast_to(pair_sym(ids, occ_ref), (16, PORTION)).astype(F32).astype(BF16)
    lane = lax.broadcasted_iota(I32, (WINDOW, LANES), 1)
    for s in range(8):
        group = jnp.bitwise_xor(hc, s)
        copies[s].wait()
        turn = load_span(windows.at[s], span, offset_of(virt_ref, group))
        block = pltpu.roll(span[...].astype(F32), turn, 1)[:, :LANES]
        rolled[:WINDOW, :] = jnp.where(lane < virt_ref[group], block, 0.0).astype(BF16)
        block = rolled[pl.ds(pl.multiple_of(starts[s] - firsts[s], 16), WINDOW), :]
        out_ref[:, s * MAIN:(s + 1) * MAIN] = block[:, :MAIN]
        out_ref[:, 8 * MAIN + s * 128:8 * MAIN + (s + 1) * 128] = block[:, MAIN:]


def terms_kernel(virt_ref, t_ref, v_ref, o0, o1, o2, o3, stack, total):
    hc = col_irrep(virt_ref)
    x, y = lax.axis_index("x"), lax.axis_index("y")
    t = t_ref[...]
    sym = jnp.broadcast_to(t[:, BMAX:BMAX + 1].astype(F32), (NX * HALF, MAIN)).astype(BF16)
    for s in range(8):
        stack[:, s * MAIN:(s + 1) * MAIN] = jnp.where(sym == jnp.asarray(s, BF16), t[:, :MAIN], jnp.zeros((), BF16))
    total[...] = lax.dot_general(v_ref[:, :8 * MAIN], stack[...], NT, preferred_element_type=F32)
    for s in range(8):

        @pl.when(virt_ref[jnp.bitwise_xor(hc, s)] > MAIN)
        def _():
            rest = jnp.where(sym[:, :128] == jnp.asarray(s, BF16), t[:, MAIN:], jnp.zeros((), BF16))
            block = v_ref[:, 8 * MAIN + s * 128:8 * MAIN + (s + 1) * 128]
            total[...] += lax.dot_general(block, rest, NT, preferred_element_type=F32)

    lane = lax.broadcasted_iota(I32, (FOLD, 128), 1)
    for k in range(NX):
        whole = k * HALF + (k % 2) * 64
        part = k * HALF + (1 - k % 2) * 128 - (k % 2) * 64
        upper, lower = total[:FOLD, part:part + 128], total[FOLD:, part:part + 128]
        if k % 2:
            upper = pltpu.roll(upper, 64, 1)
        else:
            lower = pltpu.roll(lower, 64, 1)
        folded = jnp.where(lane < 64, upper, lower).astype(BF16)
        full = total[:, whole:whole + 128].astype(BF16)
        step = lax.rem(x - k - y + 2 * NX, NY)
        for r, out_ref in enumerate((o0, o1, o2, o3)):

            @pl.when(step == r)
            def _():
                out_ref[:WINDOW, :] = full
                out_ref[WINDOW:, :] = folded


def place_kernel(virt_ref, a0, a1, a2, a3, b0, b1, b2, b3, order_ref, sym_ref, out_ref, total, wide, sem):
    ra = row_irrep(virt_ref)
    for half, refs in enumerate(((a0, a1, a2, a3), (b0, b1, b2, b3))):
        value = refs[0][...].astype(F32)
        for ref in refs[1:]:
            value += ref[...].astype(F32)
        total[:, half * 128:(half + 1) * 128] = value.astype(BF16)
    value = jnp.dot(total[:WINDOW, :], order_ref[:256, :], preferred_element_type=F32)
    upper = jnp.dot(total[WINDOW:, :], order_ref[256:512, :], preferred_element_type=F32)
    lower = jnp.dot(total[WINDOW:, :], order_ref[512:, :], preferred_element_type=F32)
    value = (value + jnp.concatenate([upper, lower], axis=0)).astype(BF16)
    sym = sym_ref[...]
    row = lax.broadcasted_iota(I32, (16, PORTION), 0)
    for group in range(8):
        offset = offset_of(virt_ref, group)
        start = block_start(offset)
        mask = sym == jnp.bitwise_xor(ra, group).astype(F32).astype(BF16)
        kept = jnp.where(jnp.concatenate([mask] * (WINDOW // 16), axis=0), value, jnp.zeros((), BF16))
        head = wide[pl.ds(start, 16), :].astype(F32)
        wide[pl.ds(start, 16), :] = jnp.where(row < offset - start, head, kept[:16].astype(F32)).astype(BF16)
        wide[pl.ds(start + 16, WINDOW - 16), :] = kept[16:]
    copy = pltpu.make_async_copy(wide.at[pl.ds(0, VIRT), :], out_ref, sem)
    copy.start()
    copy.wait()


def shift(value, axis, size, by):
    return lax.ppermute(value, axis, [(i, (i + by) % size) for i in range(size)])


def call(kernel, specs, out, scratch=(), out_specs=None, flops=0, moved=0, limit=40):
    return pl.pallas_call(
        kernel,
        in_specs=specs,
        out_specs=out_specs or jax.tree.map(lambda _: VMEM, out),
        out_shape=out,
        scratch_shapes=list(scratch),
        compiler_params=pltpu.CompilerParams(vmem_limit_bytes=limit * 2**20),
        cost_estimate=pl.CostEstimate(flops=flops, bytes_accessed=moved, transcendentals=0),
    )


def shards(virt_sizes, occ_sizes, pair_ids, amplitudes, integrals):
    shape = jax.ShapeDtypeStruct
    packed, virt, occ = call(
        pack_kernel, [HBM] * 4, (shape((HALF, LANES), BF16), shape((8,), I32), shape((8,), I32)),
        [pltpu.SMEM((8,), I32), pltpu.SMEM((8,), I32), pltpu.SMEM((PAIRS,), I32), pltpu.VMEM((ROWS, VIRT), BF16),
         pltpu.VMEM((ROWS, VIRT), F32), pltpu.VMEM((ROWS, SPAN), F32), pltpu.SemaphoreType.DMA((4,))],
        (VMEM, SMEM, SMEM), moved=300000, limit=64,
    )(virt_sizes, occ_sizes, pair_ids, amplitudes)
    mine = lax.all_to_all(packed, "z", 0, 0, tiled=True)
    across = [shift(mine, "x", NX, k) for k in (2, 1, 3)]
    blocks, order, sym, mine = call(
        blocks_kernel, [SMEM, SMEM, VMEM, HBM, VMEM],
        (shape((WINDOW, 8 * LANES), BF16), shape((6 * 128, PORTION), BF16), shape((16, PORTION), BF16),
         shape((HALF, LANES), BF16)),
        [pltpu.VMEM((8, WINDOW, VIRT), BF16), pltpu.VMEM((WINDOW, SPAN), BF16),
         pltpu.VMEM((2 * WINDOW, LANES), BF16), pltpu.SemaphoreType.DMA((8,))], moved=16000000, limit=48,
    )(virt, occ, pair_ids.reshape(NY, PORTION), integrals, mine)
    own = jnp.concatenate([mine, across[1], across[0], across[2]], axis=0)
    other = shift(own, "c", NC, 1)
    tile = shape((MESSAGE, 128), BF16)
    near, far = [], []
    for half in (own, other):
        terms = call(
            terms_kernel, [SMEM, VMEM, VMEM], (tile,) * NY,
            [pltpu.VMEM((NX * HALF, 8 * MAIN), BF16), pltpu.VMEM((WINDOW, NX * HALF), F32)],
            flops=PAIRS * WINDOW * 8 * MAIN, moved=4500000,
        )(virt, half, blocks)
        near.append(terms[0])
        far.append([shift(terms[r], "y", NY, r) for r in (2, 1, 3)])
    out = call(
        place_kernel, [SMEM] + [VMEM] * 10, shape((VIRT, PORTION), BF16),
        [pltpu.VMEM((MESSAGE, 2 * 128), BF16), pltpu.VMEM((VIRT + WINDOW, PORTION), BF16), pltpu.SemaphoreType.DMA],
        HBM, moved=2600000,
    )(virt, near[0], *far[0], near[1], *far[1], order, sym)
    return out.T


def solution(mesh):
    grid = Mesh(mesh.devices.reshape(NX, NZ, NC, NY), ("x", "z", "c", "y"))
    vp = ("x", "z", "c")
    in_specs = (P(), P(), P(), P(vp, "y"), P(vp, "y"))
    return jax.shard_map(shards, mesh=grid, in_specs=in_specs, out_specs=P("y", vp), check_vma=False)
```

```python
import functools

import jax
import jax.numpy as jnp
from jax import lax
from jax.experimental import pallas as pl
from jax.experimental.pallas import tpu as pltpu
from jax.sharding import Mesh, PartitionSpec as P

VIRT = 1600
NOCC = 200
PAIRS = 1536
BMAX = 320
NX, NZ, NC, NY = 4, 8, 2, 4
AWIDTH = VIRT // (NX * NZ * NC)
CWIDTH = VIRT // NY
ROWS = PAIRS // (NX * NZ * NC)
HALF = NZ * ROWS
PORTION = NC * HALF
LANES = 384
MAIN = 256
WINDOW = 336
FOLD = WINDOW // 2
MESSAGE = WINDOW + FOLD
SPAN = 512
LAST = 1152
META = BMAX - MAIN + 8
F32, BF16, I32 = jnp.float32, jnp.bfloat16, jnp.int32
SMEM = pl.BlockSpec(memory_space=pltpu.SMEM)
VMEM = pl.BlockSpec(memory_space=pltpu.VMEM)
HBM = pl.BlockSpec(memory_space=pltpu.HBM)
NT = (((1,), (1,)), ((), ()))


def offset_of(sizes, group):
    total = jnp.int32(0)
    for g in range(7):
        total += jnp.where(group > g, sizes[g], 0)
    return total


def size_of(sizes, group):
    total = jnp.int32(0)
    for g in range(8):
        total += jnp.where(group == g, sizes[g], 0)
    return total


def irrep_of(position, sizes):
    bound, irrep = jnp.int32(0), jnp.zeros_like(position)
    for g in range(7):
        bound += sizes[g]
        irrep += (position >= bound).astype(I32)
    return irrep


def pair_sym(ids, sizes):
    first = lax.shift_right_logical(ids * 5243, 20)
    second = ids - first * NOCC
    return jnp.bitwise_xor(irrep_of(first, sizes), irrep_of(second, sizes))


def vp_index():
    return (lax.axis_index("x") * NZ + lax.axis_index("z")) * NC + lax.axis_index("c")


def row_irrep(virt):
    return irrep_of(vp_index() * AWIDTH, virt)


def col_irrep(virt):
    return irrep_of(lax.axis_index("y") * CWIDTH, virt)


def block_start(offset):
    return pl.multiple_of(lax.div(offset, 16) * 16, 16)


def pack_kernel(virt_hbm, occ_hbm, ids_hbm, t_hbm, out_ref, virt_ref, occ_ref, ids_ref, t_ref, wide, sems):
    pairs = ((virt_hbm, virt_ref), (occ_hbm, occ_ref), (ids_hbm, ids_ref), (t_hbm, t_ref))
    copies = [pltpu.make_async_copy(a, b, sems.at[i]) for i, (a, b) in enumerate(pairs)]
    for copy in copies:
        copy.start()
    wide[:, 1536:] = jnp.zeros((ROWS, SPAN + 128), F32)
    for copy in copies[:3]:
        copy.wait()
    virt, occ = [virt_ref[g] for g in range(8)], [occ_ref[g] for g in range(8)]
    hc = col_irrep(virt)
    base = vp_index() * ROWS
    row = lax.broadcasted_iota(I32, (ROWS, 128), 0)
    lane = lax.broadcasted_iota(I32, (ROWS, 128), 1)
    ids = jnp.zeros((ROWS, 128), I32)
    for r in range(ROWS):
        ids = jnp.where(row == r, ids_ref[base + r], ids)
    sym = pair_sym(ids, occ)
    meta = jnp.where(lane < META, sym, 0)
    for g in range(8):
        meta = jnp.where(lane == META + g, lax.shift_right_logical(virt[g], 4), meta)
        meta = jnp.where(lane == META + 8 + g, jnp.bitwise_and(virt[g], 15), meta)
    parts = [jnp.zeros((ROWS, 128), F32)] * 2 + [jnp.where(lane >= BMAX - MAIN, meta, 0).astype(F32)]
    copies[3].wait()
    wide[:, :VIRT] = t_ref[...].astype(F32)
    for s in range(8):
        group = jnp.bitwise_xor(hc, s)
        offset, size = offset_of(virt, group), size_of(virt, group)
        span = wide[:, pl.ds(pl.multiple_of(lax.div(offset, 128) * 128, 128), SPAN)]
        span = pltpu.roll(span, lax.rem(SPAN - lax.rem(offset, 128), SPAN), 1)
        for i in range(3):
            keep = (sym == s) & (lane < size - i * 128)
            parts[i] = jnp.where(keep, span[:, i * 128:(i + 1) * 128], parts[i])
    packed = jnp.concatenate(parts, axis=1)
    out_ref[...] = jnp.concatenate([packed] * NZ, axis=0).astype(BF16)


def blocks_kernel(mine_ref, v_hbm, out_ref, order_ref, meta_ref, copy_ref, windows, span, sizes, sems):
    sizes[...] = mine_ref[:16, MAIN:].astype(F32).astype(I32)
    virt = [sizes[0, META + g] * 16 + sizes[0, META + 8 + g] for g in range(8)]
    ra, hc = row_irrep(virt), col_irrep(virt)
    starts = [block_start(offset_of(virt, jnp.bitwise_xor(ra, s))) for s in range(8)]
    firsts = [pl.multiple_of(jnp.minimum(start, VIRT - WINDOW), 16) for start in starts]
    copies = [
        pltpu.make_async_copy(v_hbm.at[pl.ds(firsts[s], WINDOW), :], windows.at[s, pl.ds(0, WINDOW), :], sems.at[s])
        for s in range(8)
    ]
    for copy in copies:
        copy.start()
    copy_ref[...] = mine_ref[...]
    row = lax.broadcasted_iota(I32, (8, 128), 0)
    meta = jnp.zeros((8, 128), I32)
    for g in range(8):
        meta = jnp.where(row == g, virt[g], meta)
    meta_ref[...] = meta
    column = lax.broadcasted_iota(I32, (128, PORTION), 0)
    target = lax.broadcasted_iota(I32, (128, PORTION), 1)
    for half in range(2):
        core = jnp.bitwise_xor(lax.axis_index("c"), half)

        def hits(position):
            z = lax.shift_right_logical(position * 2731, 16)
            return (z * NC + core) * ROWS + (position - z * ROWS) == target

        part = hits(jnp.bitwise_and(column, 63) + 128)
        order_ref[half * 128:half * 128 + 128, :] = hits(column).astype(F32).astype(BF16)
        order_ref[256 + half * 128:384 + half * 128, :] = (part & (column < 64)).astype(F32).astype(BF16)
        order_ref[512 + half * 128:640 + half * 128, :] = (part & (column >= 64)).astype(F32).astype(BF16)
    lane = lax.broadcasted_iota(I32, (WINDOW, LANES), 1)
    row = lax.broadcasted_iota(I32, (WINDOW, LANES), 0)
    for s in range(8):
        group = jnp.bitwise_xor(hc, s)
        offset, size = offset_of(virt, group), size_of(virt, group)
        rows = pl.ds(pl.multiple_of(starts[s] - firsts[s], 16), WINDOW)
        keep = (lane < size) & (row < VIRT - starts[s])

        def emit(value, turn):
            block = pltpu.roll(value.astype(F32), turn, 1)[:, :LANES]
            block = jnp.where(keep, block, 0.0).astype(BF16)
            out_ref[:, s * MAIN:(s + 1) * MAIN] = block[:, :MAIN]
            out_ref[:, 8 * MAIN + s * 128:8 * MAIN + (s + 1) * 128] = block[:, MAIN:]

        copies[s].wait()

        @pl.when(offset < LAST)
        def _():
            start = pl.multiple_of(lax.div(offset, 128) * 128, 128)
            emit(windows[s, rows, pl.ds(start, SPAN)], lax.rem(SPAN - lax.rem(offset, 128), SPAN))

        @pl.when(offset >= LAST)
        def _():
            span[:, :384] = windows[s, rows, LAST:1536]
            span[:, 384:448] = windows[s, rows, 1536:1600]
            span[:, 448:] = jnp.zeros((WINDOW, 64), BF16)
            emit(span[...], lax.rem(SPAN - (offset - LAST), SPAN))


def terms_kernel(steps, meta_ref, t_ref, v_ref, *refs):
    outs, (stack, tails, syms, total) = refs[:-4], refs[-4:]
    virt = [meta_ref[g, 0] for g in range(8)]
    hc = col_irrep(virt)
    x, y = lax.axis_index("x"), lax.axis_index("y")
    for i, r in enumerate(steps):
        slot = lax.rem(x - y - r + 2 * NX, NX)
        part = t_ref[pl.ds(pl.multiple_of(slot * HALF, HALF), HALF), :]
        rows = slice(i * MAIN, i * MAIN + HALF)
        sym = jnp.broadcast_to(part[:, BMAX:BMAX + 1].astype(F32), (HALF, MAIN)).astype(BF16)
        for s in range(8):
            keep = sym == jnp.asarray(s, BF16)
            stack[rows, s * MAIN:(s + 1) * MAIN] = jnp.where(keep, part[:, :MAIN], jnp.zeros((), BF16))
        tails[rows, :] = part[:, MAIN:]
        syms[rows, :] = sym[:, :128]
    total[...] = lax.dot_general(v_ref[:, :8 * MAIN], stack[...], NT, preferred_element_type=F32)
    for s in range(8):

        @pl.when(size_of(virt, jnp.bitwise_xor(hc, s)) > MAIN)
        def _():
            rest = jnp.where(syms[...] == jnp.asarray(s, BF16), tails[...], jnp.zeros((), BF16))
            block = v_ref[:, 8 * MAIN + s * 128:8 * MAIN + (s + 1) * 128]
            total[...] += lax.dot_general(block, rest, NT, preferred_element_type=F32)

    lane = lax.broadcasted_iota(I32, (FOLD, 128), 1)
    for i in range(len(steps)):
        outs[i][:WINDOW, :] = total[:, i * MAIN:i * MAIN + 128].astype(BF16)
        part = total[:, i * MAIN + 128:(i + 1) * MAIN]
        outs[i][WINDOW:, :] = jnp.where(lane < 64, part[:FOLD], pltpu.roll(part[FOLD:], 64, 1)).astype(BF16)
    if 0 in steps:
        i = steps.index(0)
        one = (lax.broadcasted_iota(I32, (16, 128), 1) == 0).astype(F32).astype(BF16)
        sym = lax.dot_general(one, syms[i * MAIN:(i + 1) * MAIN, :], NT, preferred_element_type=F32)
        outs[-1][:16, :] = sym[:, :128].astype(BF16)
        outs[-1][16:, :] = jnp.where(lane[:16] < 64, sym[:, 128:], 0.0).astype(BF16)


def place_kernel(meta_ref, a0, a1, a2, a3, b0, b1, b2, b3, sym_a, sym_b, order_ref, out_ref, total, wide, sem):
    virt = [meta_ref[g, 0] for g in range(8)]
    ra = row_irrep(virt)
    syms = jnp.concatenate([sym_a[...], sym_b[...]], axis=1)
    sym = jnp.dot(syms[:16], order_ref[:256, :], preferred_element_type=F32)
    sym += jnp.dot(syms[16:], order_ref[256:512, :], preferred_element_type=F32)
    sym = sym.astype(BF16)
    for half, refs in enumerate(((a0, a1, a2, a3), (b0, b1, b2, b3))):
        value = refs[0][...].astype(F32)
        for ref in refs[1:]:
            value += ref[...].astype(F32)
        total[:, half * 128:(half + 1) * 128] = value.astype(BF16)
    value = jnp.dot(total[:WINDOW, :], order_ref[:256, :], preferred_element_type=F32)
    upper = jnp.dot(total[WINDOW:, :], order_ref[256:512, :], preferred_element_type=F32)
    lower = jnp.dot(total[WINDOW:, :], order_ref[512:, :], preferred_element_type=F32)
    value = (value + jnp.concatenate([upper, lower], axis=0)).astype(BF16)
    row = lax.broadcasted_iota(I32, (16, PORTION), 0)
    for group in range(8):
        offset = offset_of(virt, group)
        start = block_start(offset)
        mask = sym == jnp.bitwise_xor(ra, group).astype(F32).astype(BF16)
        kept = jnp.where(jnp.concatenate([mask] * (WINDOW // 16), axis=0), value, jnp.zeros((), BF16))
        head = wide[pl.ds(start, 16), :].astype(F32)
        wide[pl.ds(start, 16), :] = jnp.where(row < offset - start, head, kept[:16].astype(F32)).astype(BF16)
        wide[pl.ds(start + 16, WINDOW - 16), :] = kept[16:]
    copy = pltpu.make_async_copy(wide.at[pl.ds(0, VIRT), :], out_ref, sem)
    copy.start()
    copy.wait()


def shift(value, axis, size, by):
    return lax.ppermute(value, axis, [(i, (i + by) % size) for i in range(size)])


def call(kernel, specs, out, scratch=(), out_specs=None, flops=0, moved=0, limit=40):
    return pl.pallas_call(
        kernel,
        in_specs=specs,
        out_specs=out_specs or jax.tree.map(lambda _: VMEM, out),
        out_shape=out,
        scratch_shapes=list(scratch),
        compiler_params=pltpu.CompilerParams(vmem_limit_bytes=limit * 2**20),
        cost_estimate=pl.CostEstimate(flops=flops, bytes_accessed=moved, transcendentals=0),
    )


def shards(virt_sizes, occ_sizes, pair_ids, amplitudes, integrals):
    shape = jax.ShapeDtypeStruct
    packed = call(
        pack_kernel, [HBM] * 4, shape((HALF, LANES), BF16),
        [pltpu.SMEM((8,), I32), pltpu.SMEM((8,), I32), pltpu.SMEM((PAIRS,), I32), pltpu.VMEM((ROWS, VIRT), BF16),
         pltpu.VMEM((ROWS, 1536 + SPAN + 128), F32), pltpu.SemaphoreType.DMA((4,))],
        moved=300000, limit=64,
    )(virt_sizes, occ_sizes, pair_ids, amplitudes)
    mine = lax.all_to_all(packed, "z", 0, 0, tiled=True)
    across = [shift(mine, "x", NX, k) for k in (2, 1, 3)]
    blocks, order, meta, mine = call(
        blocks_kernel, [VMEM, HBM],
        (shape((WINDOW, 8 * LANES), BF16), shape((6 * 128, PORTION), BF16), shape((8, 128), I32),
         shape((HALF, LANES), BF16)),
        [pltpu.VMEM((8, 2 * WINDOW, VIRT), BF16), pltpu.VMEM((WINDOW, SPAN), BF16),
         pltpu.VMEM((16, 128), I32), pltpu.SemaphoreType.DMA((8,))], moved=16000000, limit=48,
    )(mine, integrals)
    own = jnp.concatenate([mine, across[1], across[0], across[2]], axis=0)
    other = shift(own, "c", NC, 1)
    tile, sym = shape((MESSAGE, 128), BF16), shape((32, 128), BF16)
    near, far = [], []
    for half in (own, other):
        sent = {}
        for steps, out in (((2,), (tile,)), ((1, 3, 0), (tile, tile, tile, sym))):
            columns = len(steps) * MAIN
            terms = call(
                functools.partial(terms_kernel, steps), [VMEM] * 3, out,
                [pltpu.VMEM((columns, 8 * MAIN), BF16), pltpu.VMEM((columns, 128), BF16),
                 pltpu.VMEM((columns, 128), BF16), pltpu.VMEM((WINDOW, columns), F32)],
                flops=2 * columns * WINDOW * 8 * MAIN, moved=4500000,
            )(meta, half, blocks)
            for r, term in zip(steps, terms):
                sent[r] = shift(term, "y", NY, r) if r else term
        near.append(terms[-1])
        far.append([sent[r] for r in range(NY)])
    out = call(
        place_kernel, [VMEM] * 12, shape((VIRT, PORTION), BF16),
        [pltpu.VMEM((MESSAGE, 2 * 128), BF16), pltpu.VMEM((VIRT + WINDOW, PORTION), BF16), pltpu.SemaphoreType.DMA],
        HBM, moved=2600000,
    )(meta, *far[0], *far[1], *near, order)
    return out.T


def solution(mesh):
    grid = Mesh(mesh.devices.reshape(NX, NZ, NC, NY), ("x", "z", "c", "y"))
    vp = ("x", "z", "c")
    in_specs = (P(), P(), P(), P(vp, "y"), P(vp, "y"))
    return jax.shard_map(shards, mesh=grid, in_specs=in_specs, out_specs=P("y", vp), check_vma=False)
```

```python
import functools

import jax
import jax.numpy as jnp
from jax import lax
from jax.experimental import pallas as pl
from jax.experimental.pallas import tpu as pltpu
from jax.sharding import Mesh, PartitionSpec as P

VIRT = 1600
NOCC = 200
PAIRS = 1536
BMAX = 320
NX, NZ, NC, NY = 4, 8, 2, 4
AWIDTH = VIRT // (NX * NZ * NC)
CWIDTH = VIRT // NY
ROWS = PAIRS // (NX * NZ * NC)
HALF = NZ * ROWS
PORTION = NC * HALF
LANES = 384
MAIN = 256
WINDOW = 336
MESSAGE = 3 * WINDOW
SPAN = 512
LAST = 1152
META = BMAX - MAIN + 8
F32, BF16, I32 = jnp.float32, jnp.bfloat16, jnp.int32
SMEM = pl.BlockSpec(memory_space=pltpu.SMEM)
VMEM = pl.BlockSpec(memory_space=pltpu.VMEM)
HBM = pl.BlockSpec(memory_space=pltpu.HBM)
NT = (((1,), (1,)), ((), ()))


def offset_of(sizes, group):
    total = jnp.int32(0)
    for g in range(7):
        total += jnp.where(group > g, sizes[g], 0)
    return total


def size_of(sizes, group):
    total = jnp.int32(0)
    for g in range(8):
        total += jnp.where(group == g, sizes[g], 0)
    return total


def irrep_of(position, sizes):
    bound, irrep = jnp.int32(0), jnp.zeros_like(position)
    for g in range(7):
        bound += sizes[g]
        irrep += (position >= bound).astype(I32)
    return irrep


def pair_sym(ids, sizes):
    first = lax.shift_right_logical(ids * 5243, 20)
    second = ids - first * NOCC
    return jnp.bitwise_xor(irrep_of(first, sizes), irrep_of(second, sizes))


def vp_index():
    return (lax.axis_index("x") * NZ + lax.axis_index("z")) * NC + lax.axis_index("c")


def row_irrep(virt):
    return irrep_of(vp_index() * AWIDTH, virt)


def col_irrep(virt):
    return irrep_of(lax.axis_index("y") * CWIDTH, virt)


def block_start(offset):
    return pl.multiple_of(lax.div(offset, 16) * 16, 16)


def pack_kernel(virt_hbm, occ_hbm, ids_hbm, t_hbm, out_ref, virt_ref, occ_ref, ids_ref, t_ref, wide, sems):
    pairs = ((virt_hbm, virt_ref), (occ_hbm, occ_ref), (ids_hbm, ids_ref), (t_hbm, t_ref))
    copies = [pltpu.make_async_copy(a, b, sems.at[i]) for i, (a, b) in enumerate(pairs)]
    for copy in copies:
        copy.start()
    wide[:, 1536:] = jnp.zeros((ROWS, SPAN + 128), F32)
    for copy in copies[:3]:
        copy.wait()
    virt, occ = [virt_ref[g] for g in range(8)], [occ_ref[g] for g in range(8)]
    hc = col_irrep(virt)
    base = vp_index() * ROWS
    row = lax.broadcasted_iota(I32, (ROWS, 128), 0)
    lane = lax.broadcasted_iota(I32, (ROWS, 128), 1)
    ids = jnp.zeros((ROWS, 128), I32)
    for r in range(ROWS):
        ids = jnp.where(row == r, ids_ref[base + r], ids)
    sym = pair_sym(ids, occ)
    meta = jnp.where(lane < META, sym, 0)
    for g in range(8):
        meta = jnp.where(lane == META + g, lax.shift_right_logical(virt[g], 4), meta)
        meta = jnp.where(lane == META + 8 + g, jnp.bitwise_and(virt[g], 15), meta)
    parts = [jnp.zeros((ROWS, 128), F32)] * 2 + [jnp.where(lane >= BMAX - MAIN, meta, 0).astype(F32)]
    copies[3].wait()
    wide[:, :VIRT] = t_ref[...].astype(F32)
    for s in range(8):
        group = jnp.bitwise_xor(hc, s)
        offset, size = offset_of(virt, group), size_of(virt, group)
        span = wide[:, pl.ds(pl.multiple_of(lax.div(offset, 128) * 128, 128), SPAN)]
        span = pltpu.roll(span, lax.rem(SPAN - lax.rem(offset, 128), SPAN), 1)
        for i in range(3):
            keep = (sym == s) & (lane < size - i * 128)
            parts[i] = jnp.where(keep, span[:, i * 128:(i + 1) * 128], parts[i])
    packed = jnp.concatenate(parts, axis=1)
    out_ref[...] = jnp.concatenate([packed] * NZ, axis=0).astype(BF16)


def blocks_kernel(mine_ref, v_hbm, out_ref, order_ref, meta_ref, copy_ref, windows, span, sizes, sems):
    sizes[...] = mine_ref[:16, MAIN:].astype(F32).astype(I32)
    virt = [sizes[0, META + g] * 16 + sizes[0, META + 8 + g] for g in range(8)]
    ra, hc = row_irrep(virt), col_irrep(virt)
    starts = [block_start(offset_of(virt, jnp.bitwise_xor(ra, s))) for s in range(8)]
    firsts = [pl.multiple_of(jnp.minimum(start, VIRT - WINDOW), 16) for start in starts]
    copies = [
        pltpu.make_async_copy(v_hbm.at[pl.ds(firsts[s], WINDOW), :], windows.at[s, pl.ds(0, WINDOW), :], sems.at[s])
        for s in range(8)
    ]
    for copy in copies:
        copy.start()
    copy_ref[...] = mine_ref[...]
    row = lax.broadcasted_iota(I32, (8, 128), 0)
    meta = jnp.zeros((8, 128), I32)
    for g in range(8):
        meta = jnp.where(row == g, virt[g], meta)
    meta_ref[...] = meta
    column = lax.broadcasted_iota(I32, (PORTION, PORTION), 0)
    target = lax.broadcasted_iota(I32, (PORTION, PORTION), 1)
    tail = column >= 2 * 128
    other = jnp.bitwise_and(jnp.where(tail, lax.shift_right_logical(column, 6), lax.shift_right_logical(column, 7)), 1)
    position = jnp.where(tail, 128 + jnp.bitwise_and(column, 63), jnp.bitwise_and(column, 127))
    core = jnp.bitwise_xor(lax.axis_index("c"), other)
    z = lax.shift_right_logical(position * 2731, 16)
    order_ref[...] = ((z * NC + core) * ROWS + (position - z * ROWS) == target).astype(F32).astype(BF16)
    lane = lax.broadcasted_iota(I32, (WINDOW, LANES), 1)
    row = lax.broadcasted_iota(I32, (WINDOW, LANES), 0)
    for s in range(8):
        group = jnp.bitwise_xor(hc, s)
        offset, size = offset_of(virt, group), size_of(virt, group)
        rows = pl.ds(pl.multiple_of(starts[s] - firsts[s], 16), WINDOW)
        keep = (lane < size) & (row < VIRT - starts[s])

        def emit(value, turn):
            block = pltpu.roll(value.astype(F32), turn, 1)[:, :LANES]
            block = jnp.where(keep, block, 0.0).astype(BF16)
            out_ref[:, s * MAIN:(s + 1) * MAIN] = block[:, :MAIN]
            out_ref[:, 8 * MAIN + s * 128:8 * MAIN + (s + 1) * 128] = block[:, MAIN:]

        copies[s].wait()

        @pl.when(offset < LAST)
        def _():
            start = pl.multiple_of(lax.div(offset, 128) * 128, 128)
            emit(windows[s, rows, pl.ds(start, SPAN)], lax.rem(SPAN - lax.rem(offset, 128), SPAN))

        @pl.when(offset >= LAST)
        def _():
            span[:, :384] = windows[s, rows, LAST:1536]
            span[:, 384:448] = windows[s, rows, 1536:1600]
            span[:, 448:] = jnp.zeros((WINDOW, 64), BF16)
            emit(span[...], lax.rem(SPAN - (offset - LAST), SPAN))


def portion_rows(t_ref, r):
    slot = lax.rem(lax.axis_index("x") - lax.axis_index("y") - r + 2 * NX, NX)
    return t_ref[pl.ds(pl.multiple_of(slot * HALF, HALF), HALF), :]


def multiply(meta_ref, v_ref, parts, stack, tails, syms, total):
    virt = [meta_ref[g, 0] for g in range(8)]
    hc = col_irrep(virt)
    for i, part in enumerate(parts):
        rows = slice(i * MAIN, i * MAIN + HALF)
        sym = jnp.broadcast_to(part[:, BMAX:BMAX + 1].astype(F32), (HALF, MAIN)).astype(BF16)
        for s in range(8):
            keep = sym == jnp.asarray(s, BF16)
            stack[rows, s * MAIN:(s + 1) * MAIN] = jnp.where(keep, part[:, :MAIN], jnp.zeros((), BF16))
        tails[rows, :] = part[:, MAIN:]
        syms[rows, :] = sym[:, :128]
    total[...] = lax.dot_general(v_ref[:, :8 * MAIN], stack[...], NT, preferred_element_type=F32)
    for s in range(8):

        @pl.when(size_of(virt, jnp.bitwise_xor(hc, s)) > MAIN)
        def _():
            rest = jnp.where(syms[...] == jnp.asarray(s, BF16), tails[...], jnp.zeros((), BF16))
            block = v_ref[:, 8 * MAIN + s * 128:8 * MAIN + (s + 1) * 128]
            total[...] += lax.dot_general(block, rest, NT, preferred_element_type=F32)


def own_kernel(steps, meta_ref, t_ref, v_ref, *refs):
    outs, scratch = refs[:-4], refs[-4:]
    multiply(meta_ref, v_ref, [portion_rows(t_ref, r) for r in steps], *scratch)
    total = scratch[-1]
    for i, out_ref in enumerate(outs):
        out_ref[:WINDOW, :] = total[:, i * MAIN:i * MAIN + 128].astype(BF16)
        out_ref[WINDOW:, :] = total[:, i * MAIN + 128:(i + 1) * MAIN].astype(BF16)


def other_kernel(steps, after, meta_ref, t_ref, v_ref, *refs):
    refs = refs[after:]
    n = len(steps)
    mine, outs, scratch = refs[:n], refs[n:2 * n], refs[2 * n:]
    multiply(meta_ref, v_ref, [portion_rows(t_ref, r) for r in steps], *scratch)
    total = scratch[-1]
    lane = lax.broadcasted_iota(I32, (WINDOW, 128), 1)
    for i, (mine_ref, out_ref) in enumerate(zip(mine, outs)):
        out_ref[:WINDOW, :] = mine_ref[:WINDOW, :]
        out_ref[WINDOW:2 * WINDOW, :] = total[:, i * MAIN:i * MAIN + 128].astype(BF16)
        tail = pltpu.roll(total[:, i * MAIN + 128:(i + 1) * MAIN], 64, 1)
        out_ref[2 * WINDOW:, :] = jnp.where(lane < 64, mine_ref[WINDOW:, :].astype(F32), tail).astype(BF16)


def stay_kernel(meta_ref, own_ref, other_ref, v_ref, out_ref, sym_ref, *scratch):
    multiply(meta_ref, v_ref, [portion_rows(own_ref, 0), portion_rows(other_ref, 0)], *scratch)
    syms, total = scratch[-2:]
    lane = lax.broadcasted_iota(I32, (WINDOW, 128), 1)
    out_ref[:WINDOW, :] = total[:, :128].astype(BF16)
    out_ref[WINDOW:2 * WINDOW, :] = total[:, MAIN:MAIN + 128].astype(BF16)
    tail = jnp.where(lane < 64, total[:, 128:MAIN], pltpu.roll(total[:, MAIN + 128:], 64, 1))
    out_ref[2 * WINDOW:, :] = tail.astype(BF16)
    one = (lane[:16] == 0).astype(F32).astype(BF16)
    sym = lax.dot_general(one, syms[...], NT, preferred_element_type=F32)
    sym_ref[:, :128] = sym[:, :128].astype(BF16)
    sym_ref[:, 128:256] = sym[:, MAIN:MAIN + 128].astype(BF16)
    tail = jnp.where(lane[:16] < 64, sym[:, 128:MAIN], pltpu.roll(sym[:, MAIN + 128:], 64, 1))
    sym_ref[:, 256:] = tail.astype(BF16)


def place_kernel(meta_ref, a_ref, b_ref, c_ref, d_ref, sym_ref, order_ref, out_ref, total, wide, sem):
    virt = [meta_ref[g, 0] for g in range(8)]
    ra = row_irrep(virt)
    sym = jnp.dot(sym_ref[...], order_ref[...], preferred_element_type=F32).astype(BF16)
    for i in range(3):
        rows = slice(i * WINDOW, (i + 1) * WINDOW)
        value = a_ref[rows, :].astype(F32) + b_ref[rows, :].astype(F32) + c_ref[rows, :].astype(F32)
        total[:, i * 128:(i + 1) * 128] = (value + d_ref[rows, :].astype(F32)).astype(BF16)
    value = jnp.dot(total[...], order_ref[...], preferred_element_type=F32).astype(BF16)
    row = lax.broadcasted_iota(I32, (16, PORTION), 0)
    for group in range(8):
        offset = offset_of(virt, group)
        start = block_start(offset)
        mask = sym == jnp.bitwise_xor(ra, group).astype(F32).astype(BF16)
        kept = jnp.where(jnp.concatenate([mask] * (WINDOW // 16), axis=0), value, jnp.zeros((), BF16))
        head = wide[pl.ds(start, 16), :].astype(F32)
        wide[pl.ds(start, 16), :] = jnp.where(row < offset - start, head, kept[:16].astype(F32)).astype(BF16)
        wide[pl.ds(start + 16, WINDOW - 16), :] = kept[16:]
    copy = pltpu.make_async_copy(wide.at[pl.ds(0, VIRT), :], out_ref, sem)
    copy.start()
    copy.wait()


def shift(value, axis, size, by):
    return lax.ppermute(value, axis, [(i, (i + by) % size) for i in range(size)])


def call(kernel, specs, out, scratch=(), out_specs=None, flops=0, moved=0, limit=40):
    return pl.pallas_call(
        kernel,
        in_specs=specs,
        out_specs=out_specs or jax.tree.map(lambda _: VMEM, out),
        out_shape=out,
        scratch_shapes=list(scratch),
        compiler_params=pltpu.CompilerParams(vmem_limit_bytes=limit * 2**20),
        cost_estimate=pl.CostEstimate(flops=flops, bytes_accessed=moved, transcendentals=0),
    )


def shards(virt_sizes, occ_sizes, pair_ids, amplitudes, integrals):
    shape = jax.ShapeDtypeStruct
    packed = call(
        pack_kernel, [HBM] * 4, shape((HALF, LANES), BF16),
        [pltpu.SMEM((8,), I32), pltpu.SMEM((8,), I32), pltpu.SMEM((PAIRS,), I32), pltpu.VMEM((ROWS, VIRT), BF16),
         pltpu.VMEM((ROWS, 1536 + SPAN + 128), F32), pltpu.SemaphoreType.DMA((4,))],
        moved=300000, limit=64,
    )(virt_sizes, occ_sizes, pair_ids, amplitudes)
    mine = lax.all_to_all(packed, "z", 0, 0, tiled=True)
    across = [shift(mine, "x", NX, k) for k in (2, 1, 3)]
    blocks, order, meta, mine = call(
        blocks_kernel, [VMEM, HBM],
        (shape((WINDOW, 8 * LANES), BF16), shape((PORTION, PORTION), BF16), shape((8, 128), I32),
         shape((HALF, LANES), BF16)),
        [pltpu.VMEM((8, 2 * WINDOW, VIRT), BF16), pltpu.VMEM((WINDOW, SPAN), BF16),
         pltpu.VMEM((16, 128), I32), pltpu.SemaphoreType.DMA((8,))], moved=16000000, limit=48,
    )(mine, integrals)
    own = jnp.concatenate([mine, across[1], across[0], across[2]], axis=0)
    other = shift(own, "c", NC, 1)
    tile, part = shape((MESSAGE, 128), BF16), shape((2 * WINDOW, 128), BF16)

    def scratch(columns):
        return [pltpu.VMEM((columns, 8 * MAIN), BF16), pltpu.VMEM((columns, 128), BF16),
                pltpu.VMEM((columns, 128), BF16), pltpu.VMEM((WINDOW, columns), F32)]

    def cost(columns):
        return dict(flops=2 * columns * WINDOW * 8 * MAIN, moved=4000000)

    two, plus, minus = call(
        functools.partial(own_kernel, (2, 1, 3)), [VMEM] * 3, (part,) * 3, scratch(3 * MAIN), **cost(3 * MAIN)
    )(meta, own, blocks)
    far, terms = [], ()
    for steps, mine in (((2,), (two,)), ((1, 3), (plus, minus))):
        columns = len(steps) * MAIN
        operands = (meta, other, blocks, *terms, *mine)
        terms = call(
            functools.partial(other_kernel, steps, len(terms)), [VMEM] * len(operands), (tile,) * len(steps),
            scratch(columns), **cost(columns)
        )(*operands)
        far += [shift(term, "y", NY, r) for r, term in zip(steps, terms)]
    stay, sym = call(
        stay_kernel, [VMEM] * 4, (tile, shape((16, PORTION), BF16)), scratch(2 * MAIN), flops=20*10**9
    )(meta, own, other, blocks)
    out = call(
        place_kernel, [VMEM] * 7, shape((VIRT, PORTION), BF16),
        [pltpu.VMEM((WINDOW, PORTION), BF16), pltpu.VMEM((VIRT + WINDOW, PORTION), BF16), pltpu.SemaphoreType.DMA],
        HBM, moved=2600000,
    )(meta, stay, *far, sym, order)
    return out.T


def solution(mesh):
    grid = Mesh(mesh.devices.reshape(NX, NZ, NC, NY), ("x", "z", "c", "y"))
    vp = ("x", "z", "c")
    in_specs = (P(), P(), P(), P(vp, "y"), P(vp, "y"))
    return jax.shard_map(shards, mesh=grid, in_specs=in_specs, out_specs=P("y", vp), check_vma=False)
```

```python
import functools

import jax
import jax.numpy as jnp
from jax import lax
from jax.experimental import pallas as pl
from jax.experimental.pallas import tpu as pltpu
from jax.sharding import Mesh, PartitionSpec as P

VIRT = 1600
NOCC = 200
PAIRS = 1536
BMAX = 320
NX, NZ, NC, NY = 4, 8, 2, 4
AWIDTH = VIRT // (NX * NZ * NC)
CWIDTH = VIRT // NY
ROWS = PAIRS // (NX * NZ * NC)
HALF = NZ * ROWS
PORTION = NC * HALF
LANES = 384
MAIN = 256
TAIL = BMAX - MAIN
DEPTH = 8 * BMAX
WINDOW = 336
MESSAGE = 3 * WINDOW
SPAN = 512
LAST = 1152
META = BMAX - MAIN + 8
F32, BF16, I32 = jnp.float32, jnp.bfloat16, jnp.int32
SMEM = pl.BlockSpec(memory_space=pltpu.SMEM)
VMEM = pl.BlockSpec(memory_space=pltpu.VMEM)
HBM = pl.BlockSpec(memory_space=pltpu.HBM)
NT = (((1,), (1,)), ((), ()))


def offset_of(sizes, group):
    total = jnp.int32(0)
    for g in range(7):
        total += jnp.where(group > g, sizes[g], 0)
    return total


def size_of(sizes, group):
    total = jnp.int32(0)
    for g in range(8):
        total += jnp.where(group == g, sizes[g], 0)
    return total


def irrep_of(position, sizes):
    bound, irrep = jnp.int32(0), jnp.zeros_like(position)
    for g in range(7):
        bound += sizes[g]
        irrep += (position >= bound).astype(I32)
    return irrep


def pair_sym(ids, sizes):
    first = lax.shift_right_logical(ids * 5243, 20)
    second = ids - first * NOCC
    return jnp.bitwise_xor(irrep_of(first, sizes), irrep_of(second, sizes))


def vp_index():
    return (lax.axis_index("x") * NZ + lax.axis_index("z")) * NC + lax.axis_index("c")


def row_irrep(virt):
    return irrep_of(vp_index() * AWIDTH, virt)


def col_irrep(virt):
    return irrep_of(lax.axis_index("y") * CWIDTH, virt)


def block_start(offset):
    return pl.multiple_of(lax.div(offset, 16) * 16, 16)


def pack_kernel(virt_hbm, occ_hbm, ids_hbm, t_hbm, out_ref, virt_ref, occ_ref, ids_ref, t_ref, wide, sems):
    pairs = ((virt_hbm, virt_ref), (occ_hbm, occ_ref), (ids_hbm, ids_ref), (t_hbm, t_ref))
    copies = [pltpu.make_async_copy(a, b, sems.at[i]) for i, (a, b) in enumerate(pairs)]
    for copy in copies:
        copy.start()
    wide[:, 1536:] = jnp.zeros((ROWS, SPAN + 128), F32)
    for copy in copies[:3]:
        copy.wait()
    virt, occ = [virt_ref[g] for g in range(8)], [occ_ref[g] for g in range(8)]
    hc = col_irrep(virt)
    base = vp_index() * ROWS
    row = lax.broadcasted_iota(I32, (ROWS, 128), 0)
    lane = lax.broadcasted_iota(I32, (ROWS, 128), 1)
    ids = jnp.zeros((ROWS, 128), I32)
    for r in range(ROWS):
        ids = jnp.where(row == r, ids_ref[base + r], ids)
    sym = pair_sym(ids, occ)
    meta = jnp.where(lane < META, sym, 0)
    for g in range(8):
        meta = jnp.where(lane == META + g, lax.shift_right_logical(virt[g], 4), meta)
        meta = jnp.where(lane == META + 8 + g, jnp.bitwise_and(virt[g], 15), meta)
    parts = [jnp.zeros((ROWS, 128), F32)] * 2 + [jnp.where(lane >= BMAX - MAIN, meta, 0).astype(F32)]
    copies[3].wait()
    wide[:, :VIRT] = t_ref[...].astype(F32)
    for s in range(8):
        group = jnp.bitwise_xor(hc, s)
        offset, size = offset_of(virt, group), size_of(virt, group)
        span = wide[:, pl.ds(pl.multiple_of(lax.div(offset, 128) * 128, 128), SPAN)]
        span = pltpu.roll(span, lax.rem(SPAN - lax.rem(offset, 128), SPAN), 1)
        for i in range(3):
            keep = (sym == s) & (lane < size - i * 128)
            parts[i] = jnp.where(keep, span[:, i * 128:(i + 1) * 128], parts[i])
    packed = jnp.concatenate(parts, axis=1)
    out_ref[...] = jnp.concatenate([packed] * NZ, axis=0).astype(BF16)


def blocks_kernel(mine_ref, v_hbm, out_ref, order_ref, meta_ref, copy_ref, windows, span, sizes, sems):
    sizes[...] = mine_ref[:16, MAIN:].astype(F32).astype(I32)
    virt = [sizes[0, META + g] * 16 + sizes[0, META + 8 + g] for g in range(8)]
    ra, hc = row_irrep(virt), col_irrep(virt)
    starts = [block_start(offset_of(virt, jnp.bitwise_xor(ra, s))) for s in range(8)]
    firsts = [pl.multiple_of(jnp.minimum(start, VIRT - WINDOW), 16) for start in starts]
    copies = [
        pltpu.make_async_copy(v_hbm.at[pl.ds(firsts[s], WINDOW), :], windows.at[s, pl.ds(0, WINDOW), :], sems.at[s])
        for s in range(8)
    ]
    for copy in copies:
        copy.start()
    copy_ref[...] = mine_ref[...]
    row, lane = lax.broadcasted_iota(I32, (8, 128), 0), lax.broadcasted_iota(I32, (8, 128), 1)
    meta = jnp.zeros((8, 128), I32)
    for g in range(8):
        first = offset_of(virt, g)
        for i, value in enumerate((first, block_start(first), jnp.bitwise_xor(ra, g))):
            meta = jnp.where((row == g) & (lane == i), value, meta)
    meta_ref[...] = meta
    column = lax.broadcasted_iota(I32, (PORTION, PORTION), 0)
    target = lax.broadcasted_iota(I32, (PORTION, PORTION), 1)
    tail = column >= 2 * 128
    other = jnp.bitwise_and(jnp.where(tail, lax.shift_right_logical(column, 6), lax.shift_right_logical(column, 7)), 1)
    position = jnp.where(tail, 128 + jnp.bitwise_and(column, 63), jnp.bitwise_and(column, 127))
    core = jnp.bitwise_xor(lax.axis_index("c"), other)
    z = lax.shift_right_logical(position * 2731, 16)
    order_ref[...] = ((z * NC + core) * ROWS + (position - z * ROWS) == target).astype(F32).astype(BF16)
    lane = lax.broadcasted_iota(I32, (WINDOW, LANES), 1)
    row = lax.broadcasted_iota(I32, (WINDOW, LANES), 0)
    for s in range(8):
        group = jnp.bitwise_xor(hc, s)
        offset, size = offset_of(virt, group), size_of(virt, group)
        rows = pl.ds(pl.multiple_of(starts[s] - firsts[s], 16), WINDOW)
        keep = (lane < size) & (row < VIRT - starts[s])

        def emit(value, turn):
            block = pltpu.roll(value.astype(F32), turn, 1)[:, :LANES]
            block = jnp.where(keep, block, 0.0)
            out_ref[:, s * MAIN:(s + 1) * MAIN] = block[:, :MAIN].astype(BF16)
            tail, place = block[:, MAIN:], slice(8 * MAIN + s // 2 * 128, 8 * MAIN + s // 2 * 128 + 128)
            if s % 2:
                tail = out_ref[:, place].astype(F32) + pltpu.roll(tail, TAIL, 1)
            out_ref[:, place] = tail.astype(BF16)

        copies[s].wait()

        @pl.when(offset < LAST)
        def _():
            start = pl.multiple_of(lax.div(offset, 128) * 128, 128)
            emit(windows[s, rows, pl.ds(start, SPAN)], lax.rem(SPAN - lax.rem(offset, 128), SPAN))

        @pl.when(offset >= LAST)
        def _():
            span[:, :384] = windows[s, rows, LAST:1536]
            span[:, 384:448] = windows[s, rows, 1536:1600]
            span[:, 448:] = jnp.zeros((WINDOW, 64), BF16)
            emit(span[...], lax.rem(SPAN - (offset - LAST), SPAN))


def portion_rows(t_ref, r):
    slot = lax.rem(lax.axis_index("x") - lax.axis_index("y") - r + 2 * NX, NX)
    return t_ref[pl.ds(pl.multiple_of(slot * HALF, HALF), HALF), :]


def multiply(v_ref, parts, stack, syms, total):
    lane = lax.broadcasted_iota(I32, (HALF, 128), 1)
    zero = jnp.zeros((), BF16)
    for i, part in enumerate(parts):
        rows = slice(i * MAIN, i * MAIN + HALF)
        sym = jnp.broadcast_to(part[:, BMAX:BMAX + 1].astype(F32), (HALF, MAIN)).astype(BF16)
        for s in range(8):
            stack[rows, s * MAIN:(s + 1) * MAIN] = jnp.where(sym == jnp.asarray(s, BF16), part[:, :MAIN], zero)
        sym = sym[:, :128]
        tail = jnp.where(lane < TAIL, part[:, MAIN:].astype(F32), 0.0)
        turned = pltpu.roll(tail, TAIL, 1).astype(BF16)
        tail = tail.astype(BF16)
        for s in range(0, 8, 2):
            both = jnp.where(sym == jnp.asarray(s, BF16), tail, zero)
            both = jnp.where(sym == jnp.asarray(s + 1, BF16), turned, both)
            stack[rows, 8 * MAIN + s * TAIL:8 * MAIN + s * TAIL + 128] = both
        syms[rows, :] = sym
    total[...] = lax.dot_general(v_ref[...], stack[...], NT, preferred_element_type=F32)


def own_kernel(steps, t_ref, v_ref, *refs):
    outs, scratch = refs[:-3], refs[-3:]
    multiply(v_ref, [portion_rows(t_ref, r) for r in steps], *scratch)
    total = scratch[-1]
    for i, out_ref in enumerate(outs):
        out_ref[:WINDOW, :] = total[:, i * MAIN:i * MAIN + 128].astype(BF16)
        out_ref[WINDOW:, :] = total[:, i * MAIN + 128:(i + 1) * MAIN].astype(BF16)


def other_kernel(steps, after, t_ref, v_ref, *refs):
    refs = refs[after:]
    n = len(steps)
    mine, outs, scratch = refs[:n], refs[n:2 * n], refs[2 * n:]
    multiply(v_ref, [portion_rows(t_ref, r) for r in steps], *scratch)
    total = scratch[-1]
    lane = lax.broadcasted_iota(I32, (WINDOW, 128), 1)
    for i, (mine_ref, out_ref) in enumerate(zip(mine, outs)):
        out_ref[:WINDOW, :] = mine_ref[:WINDOW, :]
        out_ref[WINDOW:2 * WINDOW, :] = total[:, i * MAIN:i * MAIN + 128].astype(BF16)
        tail = pltpu.roll(total[:, i * MAIN + 128:(i + 1) * MAIN], 64, 1)
        out_ref[2 * WINDOW:, :] = jnp.where(lane < 64, mine_ref[WINDOW:, :].astype(F32), tail).astype(BF16)


def stay_kernel(own_ref, other_ref, v_ref, out_ref, sym_ref, *scratch):
    multiply(v_ref, [portion_rows(own_ref, 0), portion_rows(other_ref, 0)], *scratch)
    syms, total = scratch[-2:]
    lane = lax.broadcasted_iota(I32, (WINDOW, 128), 1)
    out_ref[:WINDOW, :] = total[:, :128].astype(BF16)
    out_ref[WINDOW:2 * WINDOW, :] = total[:, MAIN:MAIN + 128].astype(BF16)
    tail = jnp.where(lane < 64, total[:, 128:MAIN], pltpu.roll(total[:, MAIN + 128:], 64, 1))
    out_ref[2 * WINDOW:, :] = tail.astype(BF16)
    one = (lane[:16] == 0).astype(F32).astype(BF16)
    sym = lax.dot_general(one, syms[...], NT, preferred_element_type=F32)
    sym_ref[:, :128] = sym[:, :128].astype(BF16)
    sym_ref[:, 128:256] = sym[:, MAIN:MAIN + 128].astype(BF16)
    tail = jnp.where(lane[:16] < 64, sym[:, 128:MAIN], pltpu.roll(sym[:, MAIN + 128:], 64, 1))
    sym_ref[:, 256:] = tail.astype(BF16)


def place_kernel(meta_ref, a_ref, b_ref, c_ref, d_ref, sym_ref, order_ref, out_ref, total, wide, sems):
    meta = [[meta_ref[group, i] for i in range(3)] for group in range(8)]
    for i in range(3):
        rows = slice(i * WINDOW, (i + 1) * WINDOW)
        value = a_ref[rows, :].astype(F32) + b_ref[rows, :].astype(F32) + c_ref[rows, :].astype(F32)
        total[:, i * 128:(i + 1) * 128] = (value + d_ref[rows, :].astype(F32)).astype(BF16)
    row = lax.broadcasted_iota(I32, (16, 128), 0)
    copies = []
    for i in range(3):
        lanes = slice(i * 128, (i + 1) * 128)
        sym = jnp.dot(sym_ref[...], order_ref[:, lanes], preferred_element_type=F32).astype(BF16)
        value = jnp.dot(total[...], order_ref[:, lanes], preferred_element_type=F32).astype(BF16)
        for first, start, code in meta:
            start = pl.multiple_of(start, 16)
            mask = sym == code.astype(F32).astype(BF16)
            kept = jnp.where(jnp.concatenate([mask] * (WINDOW // 16), axis=0), value, jnp.zeros((), BF16))
            head = wide[pl.ds(start, 16), lanes].astype(F32)
            wide[pl.ds(start, 16), lanes] = jnp.where(row < first - start, head, kept[:16].astype(F32)).astype(BF16)
            wide[pl.ds(start + 16, WINDOW - 16), lanes] = kept[16:]
        copies.append(pltpu.make_async_copy(wide.at[pl.ds(0, VIRT), lanes], out_ref.at[:, lanes], sems.at[i]))
        copies[i].start()
    for copy in copies:
        copy.wait()


def shift(value, axis, size, by):
    return lax.ppermute(value, axis, [(i, (i + by) % size) for i in range(size)])


def call(kernel, specs, out, scratch=(), out_specs=None, flops=0, moved=0, limit=40):
    return pl.pallas_call(
        kernel,
        in_specs=specs,
        out_specs=out_specs or jax.tree.map(lambda _: VMEM, out),
        out_shape=out,
        scratch_shapes=list(scratch),
        compiler_params=pltpu.CompilerParams(vmem_limit_bytes=limit * 2**20),
        cost_estimate=pl.CostEstimate(flops=flops, bytes_accessed=moved, transcendentals=0),
    )


def shards(virt_sizes, occ_sizes, pair_ids, amplitudes, integrals):
    shape = jax.ShapeDtypeStruct
    packed = call(
        pack_kernel, [HBM] * 4, shape((HALF, LANES), BF16),
        [pltpu.SMEM((8,), I32), pltpu.SMEM((8,), I32), pltpu.SMEM((PAIRS,), I32), pltpu.VMEM((ROWS, VIRT), BF16),
         pltpu.VMEM((ROWS, 1536 + SPAN + 128), F32), pltpu.SemaphoreType.DMA((4,))],
        moved=300000, limit=64,
    )(virt_sizes, occ_sizes, pair_ids, amplitudes)
    mine = lax.all_to_all(packed, "z", 0, 0, tiled=True)
    across = [shift(mine, "x", NX, k) for k in (2, 1, 3)]
    blocks, order, meta, mine = call(
        blocks_kernel, [VMEM, HBM],
        (shape((WINDOW, DEPTH), BF16), shape((PORTION, PORTION), BF16), shape((8, 128), I32),
         shape((HALF, LANES), BF16)),
        [pltpu.VMEM((8, 2 * WINDOW, VIRT), BF16), pltpu.VMEM((WINDOW, SPAN), BF16),
         pltpu.VMEM((16, 128), I32), pltpu.SemaphoreType.DMA((8,))], moved=16000000, limit=48,
    )(mine, integrals)
    own = jnp.concatenate([mine, across[1], across[0], across[2]], axis=0)
    other = shift(own, "c", NC, 1)
    tile, part = shape((MESSAGE, 128), BF16), shape((2 * WINDOW, 128), BF16)

    def scratch(columns):
        return [pltpu.VMEM((columns, DEPTH), BF16), pltpu.VMEM((columns, 128), BF16), pltpu.VMEM((WINDOW, columns), F32)]

    def cost(columns):
        return dict(flops=2 * columns * WINDOW * DEPTH, moved=4000000)

    two, plus, minus = call(
        functools.partial(own_kernel, (2, 1, 3)), [VMEM] * 2, (part,) * 3, scratch(3 * MAIN), **cost(3 * MAIN)
    )(own, blocks)
    far, terms = [], ()
    for steps, mine in (((2,), (two,)), ((1, 3), (plus, minus))):
        columns = len(steps) * MAIN
        operands = (other, blocks, *terms, *mine)
        terms = call(
            functools.partial(other_kernel, steps, len(terms)), [VMEM] * len(operands), (tile,) * len(steps),
            scratch(columns), **cost(columns)
        )(*operands)
        far += [shift(term, "y", NY, r) for r, term in zip(steps, terms)]
    stay, sym = call(
        stay_kernel, [VMEM] * 3, (tile, shape((16, PORTION), BF16)), scratch(2 * MAIN), flops=20*10**9
    )(own, other, blocks)
    out = call(
        place_kernel, [VMEM] * 7, shape((VIRT, PORTION), BF16),
        [pltpu.VMEM((WINDOW, PORTION), BF16), pltpu.VMEM((VIRT + WINDOW, PORTION), BF16), pltpu.SemaphoreType.DMA((3,))],
        HBM, moved=2600000,
    )(meta, stay, *far, sym, order)
    return out.T


def solution(mesh):
    grid = Mesh(mesh.devices.reshape(NX, NZ, NC, NY), ("x", "z", "c", "y"))
    vp = ("x", "z", "c")
    in_specs = (P(), P(), P(), P(vp, "y"), P(vp, "y"))
    return jax.shard_map(shards, mesh=grid, in_specs=in_specs, out_specs=P("y", vp), check_vma=False)
```

```python
import functools

import jax
import jax.numpy as jnp
from jax import lax
from jax.experimental import pallas as pl
from jax.experimental.pallas import tpu as pltpu
from jax.sharding import Mesh, PartitionSpec as P

VIRT = 1600
NOCC = 200
PAIRS = 1536
BMAX = 320
NX, NZ, NC, NY = 4, 8, 2, 4
AWIDTH = VIRT // (NX * NZ * NC)
CWIDTH = VIRT // NY
ROWS = PAIRS // (NX * NZ * NC)
HALF = NZ * ROWS
PORTION = NC * HALF
LANES = 384
MAIN = 256
TAIL = BMAX - MAIN
DEPTH = 8 * BMAX
WINDOW = 336
HEIGHT = 320
MESSAGE = 3 * HEIGHT
SPAN = 512
LAST = 1152
META = BMAX - MAIN + 8
F32, BF16, I32 = jnp.float32, jnp.bfloat16, jnp.int32
SMEM = pl.BlockSpec(memory_space=pltpu.SMEM)
VMEM = pl.BlockSpec(memory_space=pltpu.VMEM)
HBM = pl.BlockSpec(memory_space=pltpu.HBM)
NT = (((1,), (1,)), ((), ()))


def offset_of(sizes, group):
    total = jnp.int32(0)
    for g in range(7):
        total += jnp.where(group > g, sizes[g], 0)
    return total


def size_of(sizes, group):
    total = jnp.int32(0)
    for g in range(8):
        total += jnp.where(group == g, sizes[g], 0)
    return total


def irrep_of(position, sizes):
    bound, irrep = jnp.int32(0), jnp.zeros_like(position)
    for g in range(7):
        bound += sizes[g]
        irrep += (position >= bound).astype(I32)
    return irrep


def pair_sym(ids, sizes):
    first = lax.shift_right_logical(ids * 5243, 20)
    second = ids - first * NOCC
    return jnp.bitwise_xor(irrep_of(first, sizes), irrep_of(second, sizes))


def vp_index():
    return (lax.axis_index("x") * NZ + lax.axis_index("z")) * NC + lax.axis_index("c")


def row_irrep(virt):
    return irrep_of(vp_index() * AWIDTH, virt)


def col_irrep(virt):
    return irrep_of(lax.axis_index("y") * CWIDTH, virt)


def block_start(offset):
    return pl.multiple_of(lax.div(offset, 16) * 16, 16)


def pack_kernel(virt_hbm, occ_hbm, ids_hbm, t_hbm, out_ref, virt_ref, occ_ref, ids_ref, t_ref, wide, sems):
    pairs = ((virt_hbm, virt_ref), (occ_hbm, occ_ref), (ids_hbm, ids_ref), (t_hbm, t_ref))
    copies = [pltpu.make_async_copy(a, b, sems.at[i]) for i, (a, b) in enumerate(pairs)]
    for copy in copies:
        copy.start()
    wide[:, 1536:] = jnp.zeros((ROWS, SPAN + 128), F32)
    for copy in copies[:3]:
        copy.wait()
    virt, occ = [virt_ref[g] for g in range(8)], [occ_ref[g] for g in range(8)]
    hc = col_irrep(virt)
    base = vp_index() * ROWS
    row = lax.broadcasted_iota(I32, (ROWS, 128), 0)
    lane = lax.broadcasted_iota(I32, (ROWS, 128), 1)
    ids = jnp.zeros((ROWS, 128), I32)
    for r in range(ROWS):
        ids = jnp.where(row == r, ids_ref[base + r], ids)
    sym = pair_sym(ids, occ)
    meta = jnp.where(lane < META, sym, 0)
    for g in range(8):
        meta = jnp.where(lane == META + g, lax.shift_right_logical(virt[g], 4), meta)
        meta = jnp.where(lane == META + 8 + g, jnp.bitwise_and(virt[g], 15), meta)
    parts = [jnp.zeros((ROWS, 128), F32)] * 2 + [jnp.where(lane >= BMAX - MAIN, meta, 0).astype(F32)]
    copies[3].wait()
    wide[:, :VIRT] = t_ref[...].astype(F32)
    for s in range(8):
        group = jnp.bitwise_xor(hc, s)
        offset, size = offset_of(virt, group), size_of(virt, group)
        span = wide[:, pl.ds(pl.multiple_of(lax.div(offset, 128) * 128, 128), SPAN)]
        span = pltpu.roll(span, lax.rem(SPAN - lax.rem(offset, 128), SPAN), 1)
        for i in range(3):
            keep = (sym == s) & (lane < size - i * 128)
            parts[i] = jnp.where(keep, span[:, i * 128:(i + 1) * 128], parts[i])
    packed = jnp.concatenate(parts, axis=1)
    out_ref[...] = jnp.concatenate([packed] * NZ, axis=0).astype(BF16)


def blocks_kernel(mine_ref, v_hbm, out_ref, order_ref, meta_ref, copy_ref, windows, span, sizes, sems):
    sizes[...] = mine_ref[:16, MAIN:].astype(F32).astype(I32)
    virt = [sizes[0, META + g] * 16 + sizes[0, META + 8 + g] for g in range(8)]
    ra, hc = row_irrep(virt), col_irrep(virt)
    offsets = [offset_of(virt, jnp.bitwise_xor(ra, s)) for s in range(8)]
    starts = [block_start(offset) for offset in offsets]
    skips = [offset - start for offset, start in zip(offsets, starts)]
    firsts = [pl.multiple_of(jnp.minimum(start, VIRT - WINDOW), 16) for start in starts]
    copies = [
        pltpu.make_async_copy(v_hbm.at[pl.ds(firsts[s], WINDOW), :], windows.at[s, pl.ds(0, WINDOW), :], sems.at[s])
        for s in range(8)
    ]
    for copy in copies:
        copy.start()
    copy_ref[...] = mine_ref[...]
    row, lane = lax.broadcasted_iota(I32, (8, 128), 0), lax.broadcasted_iota(I32, (8, 128), 1)
    meta = jnp.zeros((8, 128), I32)
    for g in range(8):
        first = offset_of(virt, g)
        for i, value in enumerate((first, block_start(first), jnp.bitwise_xor(ra, g))):
            meta = jnp.where((row == g) & (lane == i), value, meta)
    meta_ref[...] = meta
    column = lax.broadcasted_iota(I32, (PORTION, PORTION), 0)
    target = lax.broadcasted_iota(I32, (PORTION, PORTION), 1)
    tail = column >= 2 * 128
    other = jnp.bitwise_and(jnp.where(tail, lax.shift_right_logical(column, 6), lax.shift_right_logical(column, 7)), 1)
    position = jnp.where(tail, 128 + jnp.bitwise_and(column, 63), jnp.bitwise_and(column, 127))
    core = jnp.bitwise_xor(lax.axis_index("c"), other)
    z = lax.shift_right_logical(position * 2731, 16)
    order_ref[...] = ((z * NC + core) * ROWS + (position - z * ROWS) == target).astype(F32).astype(BF16)
    lane = lax.broadcasted_iota(I32, (WINDOW, LANES), 1)
    row = lax.broadcasted_iota(I32, (WINDOW, LANES), 0)
    for s in range(8):
        group = jnp.bitwise_xor(hc, s)
        offset, size = offset_of(virt, group), size_of(virt, group)
        rows = pl.ds(pl.multiple_of(starts[s] - firsts[s], 16), WINDOW)
        keep = (lane < size) & (row < VIRT - starts[s])

        def emit(value, turn):
            block = pltpu.roll(value.astype(F32), turn, 1)[:, :LANES]
            block = jnp.where(keep, block, 0.0)
            head = jnp.where(row[:16] < skips[s], block[HEIGHT:], block[:16])
            block = jnp.concatenate([head, block[16:HEIGHT]], axis=0)
            out_ref[:, s * MAIN:(s + 1) * MAIN] = block[:, :MAIN].astype(BF16)
            tail, place = block[:, MAIN:], slice(8 * MAIN + s // 2 * 128, 8 * MAIN + s // 2 * 128 + 128)
            if s % 2:
                tail = out_ref[:, place].astype(F32) + pltpu.roll(tail, TAIL, 1)
            out_ref[:, place] = tail.astype(BF16)

        copies[s].wait()

        @pl.when(offset < LAST)
        def _():
            start = pl.multiple_of(lax.div(offset, 128) * 128, 128)
            emit(windows[s, rows, pl.ds(start, SPAN)], lax.rem(SPAN - lax.rem(offset, 128), SPAN))

        @pl.when(offset >= LAST)
        def _():
            span[:, :384] = windows[s, rows, LAST:1536]
            span[:, 384:448] = windows[s, rows, 1536:1600]
            span[:, 448:] = jnp.zeros((WINDOW, 64), BF16)
            emit(span[...], lax.rem(SPAN - (offset - LAST), SPAN))


def portion_rows(t_ref, r):
    slot = lax.rem(lax.axis_index("x") - lax.axis_index("y") - r + 2 * NX, NX)
    return t_ref[pl.ds(pl.multiple_of(slot * HALF, HALF), HALF), :]


def multiply(v_ref, parts, stack, syms, total):
    lane = lax.broadcasted_iota(I32, (HALF, 128), 1)
    zero = jnp.zeros((), BF16)
    for i, part in enumerate(parts):
        rows = slice(i * MAIN, i * MAIN + HALF)
        sym = jnp.broadcast_to(part[:, BMAX:BMAX + 1].astype(F32), (HALF, MAIN)).astype(BF16)
        for s in range(8):
            stack[rows, s * MAIN:(s + 1) * MAIN] = jnp.where(sym == jnp.asarray(s, BF16), part[:, :MAIN], zero)
        sym = sym[:, :128]
        tail = jnp.where(lane < TAIL, part[:, MAIN:].astype(F32), 0.0)
        turned = pltpu.roll(tail, TAIL, 1).astype(BF16)
        tail = tail.astype(BF16)
        for s in range(0, 8, 2):
            both = jnp.where(sym == jnp.asarray(s, BF16), tail, zero)
            both = jnp.where(sym == jnp.asarray(s + 1, BF16), turned, both)
            stack[rows, 8 * MAIN + s * TAIL:8 * MAIN + s * TAIL + 128] = both
        syms[rows, :] = sym
    total[...] = lax.dot_general(v_ref[...], stack[...], NT, preferred_element_type=F32)


def own_kernel(steps, t_ref, v_ref, *refs):
    outs, scratch = refs[:-3], refs[-3:]
    multiply(v_ref, [portion_rows(t_ref, r) for r in steps], *scratch)
    total = scratch[-1]
    for i, out_ref in enumerate(outs):
        out_ref[:HEIGHT, :] = total[:, i * MAIN:i * MAIN + 128].astype(BF16)
        out_ref[HEIGHT:, :] = total[:, i * MAIN + 128:(i + 1) * MAIN].astype(BF16)


def other_kernel(steps, after, t_ref, v_ref, *refs):
    refs = refs[after:]
    n = len(steps)
    mine, outs, scratch = refs[:n], refs[n:2 * n], refs[2 * n:]
    multiply(v_ref, [portion_rows(t_ref, r) for r in steps], *scratch)
    total = scratch[-1]
    lane = lax.broadcasted_iota(I32, (HEIGHT, 128), 1)
    for i, (mine_ref, out_ref) in enumerate(zip(mine, outs)):
        out_ref[:HEIGHT, :] = mine_ref[:HEIGHT, :]
        out_ref[HEIGHT:2 * HEIGHT, :] = total[:, i * MAIN:i * MAIN + 128].astype(BF16)
        tail = pltpu.roll(total[:, i * MAIN + 128:(i + 1) * MAIN], 64, 1)
        out_ref[2 * HEIGHT:, :] = jnp.where(lane < 64, mine_ref[HEIGHT:, :].astype(F32), tail).astype(BF16)


def stay_kernel(own_ref, other_ref, v_ref, out_ref, sym_ref, *scratch):
    multiply(v_ref, [portion_rows(own_ref, 0), portion_rows(other_ref, 0)], *scratch)
    syms, total = scratch[-2:]
    lane = lax.broadcasted_iota(I32, (HEIGHT, 128), 1)
    out_ref[:HEIGHT, :] = total[:, :128].astype(BF16)
    out_ref[HEIGHT:2 * HEIGHT, :] = total[:, MAIN:MAIN + 128].astype(BF16)
    tail = jnp.where(lane < 64, total[:, 128:MAIN], pltpu.roll(total[:, MAIN + 128:], 64, 1))
    out_ref[2 * HEIGHT:, :] = tail.astype(BF16)
    one = (lane[:16] == 0).astype(F32).astype(BF16)
    sym = lax.dot_general(one, syms[...], NT, preferred_element_type=F32)
    sym_ref[:, :128] = sym[:, :128].astype(BF16)
    sym_ref[:, 128:256] = sym[:, MAIN:MAIN + 128].astype(BF16)
    tail = jnp.where(lane[:16] < 64, sym[:, 128:MAIN], pltpu.roll(sym[:, MAIN + 128:], 64, 1))
    sym_ref[:, 256:] = tail.astype(BF16)


def place_kernel(meta_ref, a_ref, b_ref, c_ref, d_ref, sym_ref, order_ref, out_ref, total, wide, sems):
    meta = [[meta_ref[group, i] for i in range(3)] for group in range(8)]
    for i in range(3):
        rows = slice(i * HEIGHT, (i + 1) * HEIGHT)
        value = a_ref[rows, :].astype(F32) + b_ref[rows, :].astype(F32) + c_ref[rows, :].astype(F32)
        total[:, i * 128:(i + 1) * 128] = (value + d_ref[rows, :].astype(F32)).astype(BF16)
    row = lax.broadcasted_iota(I32, (16, 128), 0)
    copies = []
    for i in range(3):
        lanes = slice(i * 128, (i + 1) * 128)
        sym = jnp.dot(sym_ref[...], order_ref[:, lanes], preferred_element_type=F32).astype(BF16)
        value = jnp.dot(total[...], order_ref[:, lanes], preferred_element_type=F32).astype(BF16)
        for first, start, code in meta:
            start = pl.multiple_of(start, 16)
            mask = sym == code.astype(F32).astype(BF16)
            kept = jnp.where(jnp.concatenate([mask] * (HEIGHT // 16), axis=0), value, jnp.zeros((), BF16))
            head = wide[pl.ds(start, 16), lanes].astype(F32)
            wide[pl.ds(start, 16), lanes] = jnp.where(row < first - start, head, kept[:16].astype(F32)).astype(BF16)
            wide[pl.ds(start + 16, HEIGHT - 16), lanes] = kept[16:]
            wide[pl.ds(start + HEIGHT, 16), lanes] = kept[:16]
        copies.append(pltpu.make_async_copy(wide.at[pl.ds(0, VIRT), lanes], out_ref.at[:, lanes], sems.at[i]))
        copies[i].start()
    for copy in copies:
        copy.wait()


def shift(value, axis, size, by):
    return lax.ppermute(value, axis, [(i, (i + by) % size) for i in range(size)])


def call(kernel, specs, out, scratch=(), out_specs=None, flops=0, moved=0, limit=40):
    return pl.pallas_call(
        kernel,
        in_specs=specs,
        out_specs=out_specs or jax.tree.map(lambda _: VMEM, out),
        out_shape=out,
        scratch_shapes=list(scratch),
        compiler_params=pltpu.CompilerParams(vmem_limit_bytes=limit * 2**20),
        cost_estimate=pl.CostEstimate(flops=flops, bytes_accessed=moved, transcendentals=0),
    )


def shards(virt_sizes, occ_sizes, pair_ids, amplitudes, integrals):
    shape = jax.ShapeDtypeStruct
    packed = call(
        pack_kernel, [HBM] * 4, shape((HALF, LANES), BF16),
        [pltpu.SMEM((8,), I32), pltpu.SMEM((8,), I32), pltpu.SMEM((PAIRS,), I32), pltpu.VMEM((ROWS, VIRT), BF16),
         pltpu.VMEM((ROWS, 1536 + SPAN + 128), F32), pltpu.SemaphoreType.DMA((4,))],
        moved=300000, limit=64,
    )(virt_sizes, occ_sizes, pair_ids, amplitudes)
    mine = lax.all_to_all(packed, "z", 0, 0, tiled=True)
    across = [shift(mine, "x", NX, k) for k in (2, 1, 3)]
    blocks, order, meta, mine = call(
        blocks_kernel, [VMEM, HBM],
        (shape((HEIGHT, DEPTH), BF16), shape((PORTION, PORTION), BF16), shape((8, 128), I32),
         shape((HALF, LANES), BF16)),
        [pltpu.VMEM((8, 2 * WINDOW, VIRT), BF16), pltpu.VMEM((WINDOW, SPAN), BF16),
         pltpu.VMEM((16, 128), I32), pltpu.SemaphoreType.DMA((8,))], moved=16000000, limit=48,
    )(mine, integrals)
    own = jnp.concatenate([mine, across[1], across[0], across[2]], axis=0)
    other = shift(own, "c", NC, 1)
    tile, part = shape((MESSAGE, 128), BF16), shape((2 * HEIGHT, 128), BF16)

    def scratch(columns):
        return [pltpu.VMEM((columns, DEPTH), BF16), pltpu.VMEM((columns, 128), BF16), pltpu.VMEM((HEIGHT, columns), F32)]

    def cost(columns):
        return dict(flops=2 * columns * HEIGHT * DEPTH, moved=4000000)

    two, plus, minus = call(
        functools.partial(own_kernel, (2, 1, 3)), [VMEM] * 2, (part,) * 3, scratch(3 * MAIN), **cost(3 * MAIN)
    )(own, blocks)
    far, terms = [], ()
    for steps, mine in (((2,), (two,)), ((1, 3), (plus, minus))):
        columns = len(steps) * MAIN
        operands = (other, blocks, *terms, *mine)
        terms = call(
            functools.partial(other_kernel, steps, len(terms)), [VMEM] * len(operands), (tile,) * len(steps),
            scratch(columns), **cost(columns)
        )(*operands)
        far += [shift(term, "y", NY, r) for r, term in zip(steps, terms)]
    stay, sym = call(
        stay_kernel, [VMEM] * 3, (tile, shape((16, PORTION), BF16)), scratch(2 * MAIN), flops=20*10**9
    )(own, other, blocks)
    out = call(
        place_kernel, [VMEM] * 7, shape((VIRT, PORTION), BF16),
        [pltpu.VMEM((HEIGHT, PORTION), BF16), pltpu.VMEM((VIRT + WINDOW, PORTION), BF16), pltpu.SemaphoreType.DMA((3,))],
        HBM, moved=2600000,
    )(meta, stay, *far, sym, order)
    return out.T


def solution(mesh):
    grid = Mesh(mesh.devices.reshape(NX, NZ, NC, NY), ("x", "z", "c", "y"))
    vp = ("x", "z", "c")
    in_specs = (P(), P(), P(), P(vp, "y"), P(vp, "y"))
    return jax.shard_map(shards, mesh=grid, in_specs=in_specs, out_specs=P("y", vp), check_vma=False)
```

```python
import functools

import jax
import jax.numpy as jnp
from jax import lax
from jax.experimental import pallas as pl
from jax.experimental.pallas import tpu as pltpu
from jax.sharding import Mesh, PartitionSpec as P

VIRT = 1600
NOCC = 200
PAIRS = 1536
BMAX = 320
NX, NZ, NC, NY = 4, 8, 2, 4
AWIDTH = VIRT // (NX * NZ * NC)
CWIDTH = VIRT // NY
ROWS = PAIRS // (NX * NZ * NC)
HALF = NZ * ROWS
PORTION = NC * HALF
LANES = 384
MAIN = 256
TAIL = BMAX - MAIN
DEPTH = 8 * BMAX
WINDOW = 336
HEIGHT = 320
MESSAGE = 3 * HEIGHT
SPAN = 512
LAST = 1152
PACK = 64
SLOT = NZ * PACK
META = 112
F32, BF16, I32 = jnp.float32, jnp.bfloat16, jnp.int32
SMEM = pl.BlockSpec(memory_space=pltpu.SMEM)
VMEM = pl.BlockSpec(memory_space=pltpu.VMEM)
HBM = pl.BlockSpec(memory_space=pltpu.HBM)
NT = (((1,), (1,)), ((), ()))


def offset_of(sizes, group):
    total = jnp.int32(0)
    for g in range(7):
        total += jnp.where(group > g, sizes[g], 0)
    return total


def size_of(sizes, group):
    total = jnp.int32(0)
    for g in range(8):
        total += jnp.where(group == g, sizes[g], 0)
    return total


def irrep_of(position, sizes):
    bound, irrep = jnp.int32(0), jnp.zeros_like(position)
    for g in range(7):
        bound += sizes[g]
        irrep += (position >= bound).astype(I32)
    return irrep


def pair_sym(ids, sizes):
    first = lax.shift_right_logical(ids * 5243, 20)
    second = ids - first * NOCC
    return jnp.bitwise_xor(irrep_of(first, sizes), irrep_of(second, sizes))


def vp_index():
    return (lax.axis_index("x") * NZ + lax.axis_index("z")) * NC + lax.axis_index("c")


def row_irrep(virt):
    return irrep_of(vp_index() * AWIDTH, virt)


def col_irrep(virt):
    return irrep_of(lax.axis_index("y") * CWIDTH, virt)


def block_start(offset):
    return pl.multiple_of(lax.div(offset, 16) * 16, 16)


def pack_kernel(virt_hbm, occ_hbm, ids_hbm, t_hbm, out_ref, virt_ref, occ_ref, ids_ref, t_ref, wide, sems):
    pairs = ((virt_hbm, virt_ref), (occ_hbm, occ_ref), (ids_hbm, ids_ref), (t_hbm, t_ref))
    copies = [pltpu.make_async_copy(a, b, sems.at[i]) for i, (a, b) in enumerate(pairs)]
    for copy in copies:
        copy.start()
    wide[:, 1536:] = jnp.zeros((ROWS, SPAN + 128), F32)
    for copy in copies[:3]:
        copy.wait()
    virt, occ = [virt_ref[g] for g in range(8)], [occ_ref[g] for g in range(8)]
    hc = col_irrep(virt)
    base = vp_index() * ROWS
    row = lax.broadcasted_iota(I32, (ROWS, 128), 0)
    lane = lax.broadcasted_iota(I32, (ROWS, 128), 1)
    ids = jnp.zeros((ROWS, 128), I32)
    for r in range(ROWS):
        ids = jnp.where(row == r, ids_ref[base + r], ids)
    sym = pair_sym(ids, occ)
    parts = [jnp.zeros((ROWS, 128), F32)] * 3
    copies[3].wait()
    wide[:, :VIRT] = t_ref[...].astype(F32)
    for s in range(8):
        group = jnp.bitwise_xor(hc, s)
        offset, size = offset_of(virt, group), size_of(virt, group)
        span = wide[:, pl.ds(pl.multiple_of(lax.div(offset, 128) * 128, 128), SPAN)]
        span = pltpu.roll(span, lax.rem(SPAN - lax.rem(offset, 128), SPAN), 1)
        for i in range(3):
            keep = (sym == s) & (lane < size - i * 128)
            parts[i] = jnp.where(keep, span[:, i * 128:(i + 1) * 128], parts[i])
    lane, tail = lane[:8], parts[2]
    spare = jnp.zeros((8, 128), I32)
    for i in range(3):
        spare = jnp.where((lane >= 64 + 16 * i) & (lane < 80 + 16 * i), sym[8 * i:8 * i + 8], spare)
    for g in range(8):
        spare = jnp.where(lane == META + g, lax.shift_right_logical(virt[g], 4), spare)
        spare = jnp.where(lane == META + 8 + g, jnp.bitwise_and(virt[g], 15), spare)
    first = jnp.where(lane < TAIL, tail[:8], pltpu.roll(tail[16:], TAIL, 1))
    second = jnp.where(lane < TAIL, tail[8:16], spare.astype(F32))
    packed = jnp.concatenate([parts[0], parts[1], first, second], axis=0)
    out_ref[...] = jnp.concatenate([packed] * NZ, axis=0).astype(BF16)


def blocks_kernel(mine_ref, v_hbm, out_ref, order_ref, meta_ref, copy_ref, windows, span, sizes, sems):
    sizes[...] = mine_ref[PACK - 16:PACK, :].astype(F32).astype(I32)
    virt = [sizes[8, META + g] * 16 + sizes[8, META + 8 + g] for g in range(8)]
    ra, hc = row_irrep(virt), col_irrep(virt)
    offsets = [offset_of(virt, jnp.bitwise_xor(ra, s)) for s in range(8)]
    starts = [block_start(offset) for offset in offsets]
    skips = [offset - start for offset, start in zip(offsets, starts)]
    firsts = [pl.multiple_of(jnp.minimum(start, VIRT - WINDOW), 16) for start in starts]
    copies = [
        pltpu.make_async_copy(v_hbm.at[pl.ds(firsts[s], WINDOW), :], windows.at[s, pl.ds(0, WINDOW), :], sems.at[s])
        for s in range(8)
    ]
    for copy in copies:
        copy.start()
    copy_ref[...] = mine_ref[...]
    row, lane = lax.broadcasted_iota(I32, (8, 128), 0), lax.broadcasted_iota(I32, (8, 128), 1)
    meta = jnp.zeros((8, 128), I32)
    for g in range(8):
        first = offset_of(virt, g)
        for i, value in enumerate((first, block_start(first), jnp.bitwise_xor(ra, g))):
            meta = jnp.where((row == g) & (lane == i), value, meta)
    meta_ref[...] = meta
    column = lax.broadcasted_iota(I32, (PORTION, PORTION), 0)
    target = lax.broadcasted_iota(I32, (PORTION, PORTION), 1)
    tail = column >= 2 * 128
    other = jnp.bitwise_and(jnp.where(tail, lax.shift_right_logical(column, 6), lax.shift_right_logical(column, 7)), 1)
    position = jnp.where(tail, 128 + jnp.bitwise_and(column, 63), jnp.bitwise_and(column, 127))
    core = jnp.bitwise_xor(lax.axis_index("c"), other)
    z = lax.shift_right_logical(position * 2731, 16)
    order_ref[...] = ((z * NC + core) * ROWS + (position - z * ROWS) == target).astype(F32).astype(BF16)
    lane = lax.broadcasted_iota(I32, (WINDOW, LANES), 1)
    row = lax.broadcasted_iota(I32, (WINDOW, LANES), 0)
    for s in range(8):
        group = jnp.bitwise_xor(hc, s)
        offset, size = offset_of(virt, group), size_of(virt, group)
        rows = pl.ds(pl.multiple_of(starts[s] - firsts[s], 16), WINDOW)
        keep = (lane < size) & (row < VIRT - starts[s])

        def emit(value, turn):
            block = pltpu.roll(value.astype(F32), turn, 1)[:, :LANES]
            block = jnp.where(keep, block, 0.0)
            head = jnp.where(row[:16] < skips[s], block[HEIGHT:], block[:16])
            block = jnp.concatenate([head, block[16:HEIGHT]], axis=0)
            out_ref[:, s * MAIN:(s + 1) * MAIN] = block[:, :MAIN].astype(BF16)
            tail, place = block[:, MAIN:], slice(8 * MAIN + s // 2 * 128, 8 * MAIN + s // 2 * 128 + 128)
            if s % 2:
                tail = out_ref[:, place].astype(F32) + pltpu.roll(tail, TAIL, 1)
            out_ref[:, place] = tail.astype(BF16)

        copies[s].wait()

        @pl.when(offset < LAST)
        def _():
            start = pl.multiple_of(lax.div(offset, 128) * 128, 128)
            emit(windows[s, rows, pl.ds(start, SPAN)], lax.rem(SPAN - lax.rem(offset, 128), SPAN))

        @pl.when(offset >= LAST)
        def _():
            span[:, :384] = windows[s, rows, LAST:1536]
            span[:, 384:448] = windows[s, rows, 1536:1600]
            span[:, 448:] = jnp.zeros((WINDOW, 64), BF16)
            emit(span[...], lax.rem(SPAN - (offset - LAST), SPAN))


def portion_rows(t_ref, r):
    slot = lax.rem(lax.axis_index("x") - lax.axis_index("y") - r + 2 * NX, NX)
    return t_ref[pl.ds(pl.multiple_of(slot * SLOT, SLOT), SLOT), :]


def multiply(v_ref, parts, stack, syms, total):
    lane = lax.broadcasted_iota(I32, (HALF, 128), 1)
    zero = jnp.zeros((), BF16)
    for i, part in enumerate(parts):
        rows = slice(i * MAIN, i * MAIN + HALF)
        part = part.astype(F32)
        blocks = [part[z * PACK:(z + 1) * PACK] for z in range(NZ)]
        halves = [jnp.concatenate([b[h * ROWS:(h + 1) * ROWS] for b in blocks], axis=0).astype(BF16) for h in range(2)]
        columns = [b[56:, 64 + 16 * k:65 + 16 * k] for b in blocks for k in range(3)]
        sym = jnp.concatenate([jnp.broadcast_to(c, (8, 128)) for c in columns], axis=0).astype(BF16)
        for s in range(8):
            keep = sym == jnp.asarray(s, BF16)
            for h in range(2):
                stack[rows, s * MAIN + h * 128:s * MAIN + h * 128 + 128] = jnp.where(keep, halves[h], zero)
        tail = jnp.concatenate([t for b in blocks for t in (b[48:], pltpu.roll(b[48:56], TAIL, 1))], axis=0)
        tail = jnp.where(lane < TAIL, tail, 0.0)
        turned = pltpu.roll(tail, TAIL, 1).astype(BF16)
        tail = tail.astype(BF16)
        for s in range(0, 8, 2):
            both = jnp.where(sym == jnp.asarray(s, BF16), tail, zero)
            both = jnp.where(sym == jnp.asarray(s + 1, BF16), turned, both)
            stack[rows, 8 * MAIN + s * TAIL:8 * MAIN + s * TAIL + 128] = both
        syms[rows, :] = sym
    total[...] = lax.dot_general(v_ref[...], stack[...], NT, preferred_element_type=F32)


def own_kernel(steps, t_ref, v_ref, *refs):
    outs, scratch = refs[:-3], refs[-3:]
    multiply(v_ref, [portion_rows(t_ref, r) for r in steps], *scratch)
    total = scratch[-1]
    for i, out_ref in enumerate(outs):
        out_ref[:HEIGHT, :] = total[:, i * MAIN:i * MAIN + 128].astype(BF16)
        out_ref[HEIGHT:, :] = total[:, i * MAIN + 128:(i + 1) * MAIN].astype(BF16)


def other_kernel(steps, after, t_ref, v_ref, *refs):
    refs = refs[after:]
    n = len(steps)
    mine, outs, scratch = refs[:n], refs[n:2 * n], refs[2 * n:]
    multiply(v_ref, [portion_rows(t_ref, r) for r in steps], *scratch)
    total = scratch[-1]
    lane = lax.broadcasted_iota(I32, (HEIGHT, 128), 1)
    for i, (mine_ref, out_ref) in enumerate(zip(mine, outs)):
        out_ref[:HEIGHT, :] = mine_ref[:HEIGHT, :]
        out_ref[HEIGHT:2 * HEIGHT, :] = total[:, i * MAIN:i * MAIN + 128].astype(BF16)
        tail = pltpu.roll(total[:, i * MAIN + 128:(i + 1) * MAIN], 64, 1)
        out_ref[2 * HEIGHT:, :] = jnp.where(lane < 64, mine_ref[HEIGHT:, :].astype(F32), tail).astype(BF16)


def stay_kernel(own_ref, other_ref, v_ref, out_ref, sym_ref, *scratch):
    multiply(v_ref, [portion_rows(own_ref, 0), portion_rows(other_ref, 0)], *scratch)
    syms, total = scratch[-2:]
    lane = lax.broadcasted_iota(I32, (HEIGHT, 128), 1)
    out_ref[:HEIGHT, :] = total[:, :128].astype(BF16)
    out_ref[HEIGHT:2 * HEIGHT, :] = total[:, MAIN:MAIN + 128].astype(BF16)
    tail = jnp.where(lane < 64, total[:, 128:MAIN], pltpu.roll(total[:, MAIN + 128:], 64, 1))
    out_ref[2 * HEIGHT:, :] = tail.astype(BF16)
    one = (lane[:16] == 0).astype(F32).astype(BF16)
    sym = lax.dot_general(one, syms[...], NT, preferred_element_type=F32)
    sym_ref[:, :128] = sym[:, :128].astype(BF16)
    sym_ref[:, 128:256] = sym[:, MAIN:MAIN + 128].astype(BF16)
    tail = jnp.where(lane[:16] < 64, sym[:, 128:MAIN], pltpu.roll(sym[:, MAIN + 128:], 64, 1))
    sym_ref[:, 256:] = tail.astype(BF16)


def place_kernel(meta_ref, a_ref, b_ref, c_ref, d_ref, sym_ref, order_ref, out_ref, total, wide, sems):
    meta = [[meta_ref[group, i] for i in range(3)] for group in range(8)]
    for i in range(3):
        rows = slice(i * HEIGHT, (i + 1) * HEIGHT)
        value = a_ref[rows, :].astype(F32) + b_ref[rows, :].astype(F32) + c_ref[rows, :].astype(F32)
        total[:, i * 128:(i + 1) * 128] = (value + d_ref[rows, :].astype(F32)).astype(BF16)
    row = lax.broadcasted_iota(I32, (16, 128), 0)
    copies = []
    for i in range(3):
        lanes = slice(i * 128, (i + 1) * 128)
        sym = jnp.dot(sym_ref[...], order_ref[:, lanes], preferred_element_type=F32).astype(BF16)
        value = jnp.dot(total[...], order_ref[:, lanes], preferred_element_type=F32).astype(BF16)
        for first, start, code in meta:
            start = pl.multiple_of(start, 16)
            mask = sym == code.astype(F32).astype(BF16)
            kept = jnp.where(jnp.concatenate([mask] * (HEIGHT // 16), axis=0), value, jnp.zeros((), BF16))
            head = wide[pl.ds(start, 16), lanes].astype(F32)
            wide[pl.ds(start, 16), lanes] = jnp.where(row < first - start, head, kept[:16].astype(F32)).astype(BF16)
            wide[pl.ds(start + 16, HEIGHT - 16), lanes] = kept[16:]
            wide[pl.ds(start + HEIGHT, 16), lanes] = kept[:16]
        copies.append(pltpu.make_async_copy(wide.at[pl.ds(0, VIRT), lanes], out_ref.at[:, lanes], sems.at[i]))
        copies[i].start()
    for copy in copies:
        copy.wait()


def shift(value, axis, size, by):
    return lax.ppermute(value, axis, [(i, (i + by) % size) for i in range(size)])


def call(kernel, specs, out, scratch=(), out_specs=None, flops=0, moved=0, limit=40):
    return pl.pallas_call(
        kernel,
        in_specs=specs,
        out_specs=out_specs or jax.tree.map(lambda _: VMEM, out),
        out_shape=out,
        scratch_shapes=list(scratch),
        compiler_params=pltpu.CompilerParams(vmem_limit_bytes=limit * 2**20),
        cost_estimate=pl.CostEstimate(flops=flops, bytes_accessed=moved, transcendentals=0),
    )


def shards(virt_sizes, occ_sizes, pair_ids, amplitudes, integrals):
    shape = jax.ShapeDtypeStruct
    packed = call(
        pack_kernel, [HBM] * 4, shape((SLOT, 128), BF16),
        [pltpu.SMEM((8,), I32), pltpu.SMEM((8,), I32), pltpu.SMEM((PAIRS,), I32), pltpu.VMEM((ROWS, VIRT), BF16),
         pltpu.VMEM((ROWS, 1536 + SPAN + 128), F32), pltpu.SemaphoreType.DMA((4,))],
        moved=300000, limit=64,
    )(virt_sizes, occ_sizes, pair_ids, amplitudes)
    mine = lax.all_to_all(packed, "z", 0, 0, tiled=True)
    across = [shift(mine, "x", NX, k) for k in (2, 1, 3)]
    blocks, order, meta, mine = call(
        blocks_kernel, [VMEM, HBM],
        (shape((HEIGHT, DEPTH), BF16), shape((PORTION, PORTION), BF16), shape((8, 128), I32),
         shape((SLOT, 128), BF16)),
        [pltpu.VMEM((8, 2 * WINDOW, VIRT), BF16), pltpu.VMEM((WINDOW, SPAN), BF16),
         pltpu.VMEM((16, 128), I32), pltpu.SemaphoreType.DMA((8,))], moved=16000000, limit=48,
    )(mine, integrals)
    own = jnp.concatenate([mine, across[1], across[0], across[2]], axis=0)
    other = shift(own, "c", NC, 1)
    tile, part = shape((MESSAGE, 128), BF16), shape((2 * HEIGHT, 128), BF16)

    def scratch(columns):
        return [pltpu.VMEM((columns, DEPTH), BF16), pltpu.VMEM((columns, 128), BF16), pltpu.VMEM((HEIGHT, columns), F32)]

    def cost(columns):
        return dict(flops=2 * columns * HEIGHT * DEPTH, moved=4000000)

    two, plus, minus = call(
        functools.partial(own_kernel, (2, 1, 3)), [VMEM] * 2, (part,) * 3, scratch(3 * MAIN), **cost(3 * MAIN)
    )(own, blocks)
    far, terms = [], ()
    for steps, mine in (((2,), (two,)), ((1, 3), (plus, minus))):
        columns = len(steps) * MAIN
        operands = (other, blocks, *terms, *mine)
        terms = call(
            functools.partial(other_kernel, steps, len(terms)), [VMEM] * len(operands), (tile,) * len(steps),
            scratch(columns), **cost(columns)
        )(*operands)
        far += [shift(term, "y", NY, r) for r, term in zip(steps, terms)]
    stay, sym = call(
        stay_kernel, [VMEM] * 3, (tile, shape((16, PORTION), BF16)), scratch(2 * MAIN), flops=20*10**9
    )(own, other, blocks)
    out = call(
        place_kernel, [VMEM] * 7, shape((VIRT, PORTION), BF16),
        [pltpu.VMEM((HEIGHT, PORTION), BF16), pltpu.VMEM((VIRT + WINDOW, PORTION), BF16), pltpu.SemaphoreType.DMA((3,))],
        HBM, moved=2600000,
    )(meta, stay, *far, sym, order)
    return out.T


def solution(mesh):
    grid = Mesh(mesh.devices.reshape(NX, NZ, NC, NY), ("x", "z", "c", "y"))
    vp = ("x", "z", "c")
    in_specs = (P(), P(), P(), P(vp, "y"), P(vp, "y"))
    return jax.shard_map(shards, mesh=grid, in_specs=in_specs, out_specs=P("y", vp), check_vma=False)
```

```python
import functools

import jax
import jax.numpy as jnp
from jax import lax
from jax.experimental import pallas as pl
from jax.experimental.pallas import tpu as pltpu
from jax.sharding import Mesh, PartitionSpec as P

VIRT = 1600
NOCC = 200
PAIRS = 1536
BMAX = 320
NX, NZ, NC, NY = 4, 8, 2, 4
AWIDTH = VIRT // (NX * NZ * NC)
CWIDTH = VIRT // NY
ROWS = PAIRS // (NX * NZ * NC)
HALF = NZ * ROWS
PORTION = NC * HALF
LANES = 384
MAIN = 256
TAIL = BMAX - MAIN
DEPTH = 8 * BMAX
WINDOW = 336
HEIGHT = 320
MESSAGE = 3 * HEIGHT
SPAN = 512
LAST = 1152
PACK = 64
SLOT = NZ * PACK
META = 112
F32, BF16, I32 = jnp.float32, jnp.bfloat16, jnp.int32
SMEM = pl.BlockSpec(memory_space=pltpu.SMEM)
VMEM = pl.BlockSpec(memory_space=pltpu.VMEM)
HBM = pl.BlockSpec(memory_space=pltpu.HBM)
NT = (((1,), (1,)), ((), ()))


def offset_of(sizes, group):
    total = jnp.int32(0)
    for g in range(7):
        total += jnp.where(group > g, sizes[g], 0)
    return total


def size_of(sizes, group):
    total = jnp.int32(0)
    for g in range(8):
        total += jnp.where(group == g, sizes[g], 0)
    return total


def irrep_of(position, sizes):
    bound, irrep = jnp.int32(0), jnp.zeros_like(position)
    for g in range(7):
        bound += sizes[g]
        irrep += (position >= bound).astype(I32)
    return irrep


def pair_sym(ids, sizes):
    first = lax.shift_right_logical(ids * 5243, 20)
    second = ids - first * NOCC
    return jnp.bitwise_xor(irrep_of(first, sizes), irrep_of(second, sizes))


def vp_index():
    return (lax.axis_index("x") * NZ + lax.axis_index("z")) * NC + lax.axis_index("c")


def row_irrep(virt):
    return irrep_of(vp_index() * AWIDTH, virt)


def col_irrep(virt):
    return irrep_of(lax.axis_index("y") * CWIDTH, virt)


def block_start(offset):
    return pl.multiple_of(lax.div(offset, 16) * 16, 16)


def pack_kernel(virt_hbm, occ_hbm, ids_hbm, t_hbm, out_ref, virt_ref, occ_ref, ids_ref, t_ref, wide, sems):
    pairs = ((virt_hbm, virt_ref), (occ_hbm, occ_ref), (ids_hbm, ids_ref), (t_hbm, t_ref))
    copies = [pltpu.make_async_copy(a, b, sems.at[i]) for i, (a, b) in enumerate(pairs)]
    for copy in copies:
        copy.start()
    wide[:, 1536:] = jnp.zeros((ROWS, SPAN + 128), F32)
    for copy in copies[:3]:
        copy.wait()
    virt, occ = [virt_ref[g] for g in range(8)], [occ_ref[g] for g in range(8)]
    hc = col_irrep(virt)
    base = vp_index() * ROWS
    row = lax.broadcasted_iota(I32, (ROWS, 128), 0)
    lane = lax.broadcasted_iota(I32, (ROWS, 128), 1)
    ids = jnp.zeros((ROWS, 128), I32)
    for r in range(ROWS):
        ids = jnp.where(row == r, ids_ref[base + r], ids)
    sym = pair_sym(ids, occ)
    parts = [jnp.zeros((ROWS, 128), F32)] * 3
    copies[3].wait()
    wide[:, :VIRT] = t_ref[...].astype(F32)
    for s in range(8):
        group = jnp.bitwise_xor(hc, s)
        offset, size = offset_of(virt, group), size_of(virt, group)
        span = wide[:, pl.ds(pl.multiple_of(lax.div(offset, 128) * 128, 128), SPAN)]
        span = pltpu.roll(span, lax.rem(SPAN - lax.rem(offset, 128), SPAN), 1)
        for i in range(3):
            keep = (sym == s) & (lane < size - i * 128)
            parts[i] = jnp.where(keep, span[:, i * 128:(i + 1) * 128], parts[i])
    lane, tail = lane[:8], parts[2]
    spare = jnp.zeros((8, 128), I32)
    for i in range(3):
        spare = jnp.where((lane >= 64 + 16 * i) & (lane < 80 + 16 * i), sym[8 * i:8 * i + 8], spare)
    for g in range(8):
        spare = jnp.where(lane == META + g, lax.shift_right_logical(virt[g], 4), spare)
        spare = jnp.where(lane == META + 8 + g, jnp.bitwise_and(virt[g], 15), spare)
    first = jnp.where(lane < TAIL, tail[:8], pltpu.roll(tail[16:], TAIL, 1))
    second = jnp.where(lane < TAIL, tail[8:16], spare.astype(F32))
    packed = jnp.concatenate([parts[0], parts[1], first, second], axis=0)
    out_ref[...] = jnp.concatenate([packed] * NZ, axis=0).astype(BF16)


def blocks_kernel(mine_ref, v_hbm, out_ref, order_ref, meta_ref, copy_ref, windows, span, sizes, sems):
    sizes[...] = mine_ref[PACK - 16:PACK, :].astype(F32).astype(I32)
    virt = [sizes[8, META + g] * 16 + sizes[8, META + 8 + g] for g in range(8)]
    ra, hc = row_irrep(virt), col_irrep(virt)
    offsets = [offset_of(virt, jnp.bitwise_xor(ra, s)) for s in range(8)]
    starts = [block_start(offset) for offset in offsets]
    skips = [offset - start for offset, start in zip(offsets, starts)]
    firsts = [pl.multiple_of(jnp.minimum(start, VIRT - WINDOW), 16) for start in starts]
    spans = [offset_of(virt, jnp.bitwise_xor(hc, s)) for s in range(8)]

    def fetch(s, whole):
        lanes, place = pl.ds(pl.multiple_of(lax.div(spans[s], 128) * 128, 128), SPAN), pl.ds(0, SPAN)
        if whole:
            lanes = place = slice(None)
        source = v_hbm.at[pl.ds(firsts[s], WINDOW), lanes]
        return pltpu.make_async_copy(source, windows.at[s, pl.ds(0, WINDOW), place], sems.at[s])

    for s in range(8):
        pl.when(spans[s] < LAST)(lambda: fetch(s, False).start())
        pl.when(spans[s] >= LAST)(lambda: fetch(s, True).start())
    copy_ref[...] = mine_ref[...]
    row, lane = lax.broadcasted_iota(I32, (8, 128), 0), lax.broadcasted_iota(I32, (8, 128), 1)
    meta = jnp.zeros((8, 128), I32)
    for g in range(8):
        first = offset_of(virt, g)
        for i, value in enumerate((first, block_start(first), jnp.bitwise_xor(ra, g))):
            meta = jnp.where((row == g) & (lane == i), value, meta)
    meta_ref[...] = meta
    column = lax.broadcasted_iota(I32, (PORTION, PORTION), 0)
    target = lax.broadcasted_iota(I32, (PORTION, PORTION), 1)
    tail = column >= 2 * 128
    other = jnp.bitwise_and(jnp.where(tail, lax.shift_right_logical(column, 6), lax.shift_right_logical(column, 7)), 1)
    position = jnp.where(tail, 128 + jnp.bitwise_and(column, 63), jnp.bitwise_and(column, 127))
    core = jnp.bitwise_xor(lax.axis_index("c"), other)
    z = lax.shift_right_logical(position * 2731, 16)
    order_ref[...] = ((z * NC + core) * ROWS + (position - z * ROWS) == target).astype(F32).astype(BF16)
    lane = lax.broadcasted_iota(I32, (WINDOW, LANES), 1)
    row = lax.broadcasted_iota(I32, (WINDOW, LANES), 0)
    for s in range(8):
        group = jnp.bitwise_xor(hc, s)
        offset, size = spans[s], size_of(virt, group)
        rows = pl.ds(pl.multiple_of(starts[s] - firsts[s], 16), WINDOW)
        keep = (lane < size) & (row < VIRT - starts[s])

        def emit(value, turn):
            block = pltpu.roll(value.astype(F32), turn, 1)[:, :LANES]
            block = jnp.where(keep, block, 0.0)
            head = jnp.where(row[:16] < skips[s], block[HEIGHT:], block[:16])
            block = jnp.concatenate([head, block[16:HEIGHT]], axis=0)
            out_ref[:, s * MAIN:(s + 1) * MAIN] = block[:, :MAIN].astype(BF16)
            tail, place = block[:, MAIN:], slice(8 * MAIN + s // 2 * 128, 8 * MAIN + s // 2 * 128 + 128)
            if s % 2:
                tail = out_ref[:, place].astype(F32) + pltpu.roll(tail, TAIL, 1)
            out_ref[:, place] = tail.astype(BF16)

        @pl.when(offset < LAST)
        def _():
            fetch(s, False).wait()
            emit(windows[s, rows, :SPAN], lax.rem(SPAN - lax.rem(offset, 128), SPAN))

        @pl.when(offset >= LAST)
        def _():
            fetch(s, True).wait()
            span[:, :384] = windows[s, rows, LAST:1536]
            span[:, 384:448] = windows[s, rows, 1536:1600]
            span[:, 448:] = jnp.zeros((WINDOW, 64), BF16)
            emit(span[...], lax.rem(SPAN - (offset - LAST), SPAN))


def portion_rows(t_ref, r):
    slot = lax.rem(lax.axis_index("x") - lax.axis_index("y") - r + 2 * NX, NX)
    return t_ref[pl.ds(pl.multiple_of(slot * SLOT, SLOT), SLOT), :]


def multiply(v_ref, parts, stack, syms, total):
    lane = lax.broadcasted_iota(I32, (HALF, 128), 1)
    zero = jnp.zeros((), BF16)
    for i, part in enumerate(parts):
        rows = slice(i * MAIN, i * MAIN + HALF)
        part = part.astype(F32)
        blocks = [part[z * PACK:(z + 1) * PACK] for z in range(NZ)]
        halves = [jnp.concatenate([b[h * ROWS:(h + 1) * ROWS] for b in blocks], axis=0).astype(BF16) for h in range(2)]
        columns = [b[56:, 64 + 16 * k:65 + 16 * k] for b in blocks for k in range(3)]
        sym = jnp.concatenate([jnp.broadcast_to(c, (8, 128)) for c in columns], axis=0).astype(BF16)
        for s in range(8):
            keep = sym == jnp.asarray(s, BF16)
            for h in range(2):
                stack[rows, s * MAIN + h * 128:s * MAIN + h * 128 + 128] = jnp.where(keep, halves[h], zero)
        tail = jnp.concatenate([t for b in blocks for t in (b[48:], pltpu.roll(b[48:56], TAIL, 1))], axis=0)
        tail = jnp.where(lane < TAIL, tail, 0.0)
        turned = pltpu.roll(tail, TAIL, 1).astype(BF16)
        tail = tail.astype(BF16)
        for s in range(0, 8, 2):
            both = jnp.where(sym == jnp.asarray(s, BF16), tail, zero)
            both = jnp.where(sym == jnp.asarray(s + 1, BF16), turned, both)
            stack[rows, 8 * MAIN + s * TAIL:8 * MAIN + s * TAIL + 128] = both
        syms[rows, :] = sym
    total[...] = lax.dot_general(v_ref[...], stack[...], NT, preferred_element_type=F32)


def own_kernel(steps, t_ref, v_ref, *refs):
    outs, scratch = refs[:-3], refs[-3:]
    multiply(v_ref, [portion_rows(t_ref, r) for r in steps], *scratch)
    total = scratch[-1]
    for i, out_ref in enumerate(outs):
        out_ref[:HEIGHT, :] = total[:, i * MAIN:i * MAIN + 128].astype(BF16)
        out_ref[HEIGHT:, :] = total[:, i * MAIN + 128:(i + 1) * MAIN].astype(BF16)


def other_kernel(steps, after, t_ref, v_ref, *refs):
    refs = refs[after:]
    n = len(steps)
    mine, outs, scratch = refs[:n], refs[n:2 * n], refs[2 * n:]
    multiply(v_ref, [portion_rows(t_ref, r) for r in steps], *scratch)
    total = scratch[-1]
    lane = lax.broadcasted_iota(I32, (HEIGHT, 128), 1)
    for i, (mine_ref, out_ref) in enumerate(zip(mine, outs)):
        out_ref[:HEIGHT, :] = mine_ref[:HEIGHT, :]
        out_ref[HEIGHT:2 * HEIGHT, :] = total[:, i * MAIN:i * MAIN + 128].astype(BF16)
        tail = pltpu.roll(total[:, i * MAIN + 128:(i + 1) * MAIN], 64, 1)
        out_ref[2 * HEIGHT:, :] = jnp.where(lane < 64, mine_ref[HEIGHT:, :].astype(F32), tail).astype(BF16)


def stay_kernel(own_ref, other_ref, v_ref, out_ref, sym_ref, *scratch):
    multiply(v_ref, [portion_rows(own_ref, 0), portion_rows(other_ref, 0)], *scratch)
    syms, total = scratch[-2:]
    lane = lax.broadcasted_iota(I32, (HEIGHT, 128), 1)
    out_ref[:HEIGHT, :] = total[:, :128].astype(BF16)
    out_ref[HEIGHT:2 * HEIGHT, :] = total[:, MAIN:MAIN + 128].astype(BF16)
    tail = jnp.where(lane < 64, total[:, 128:MAIN], pltpu.roll(total[:, MAIN + 128:], 64, 1))
    out_ref[2 * HEIGHT:, :] = tail.astype(BF16)
    one = (lane[:16] == 0).astype(F32).astype(BF16)
    sym = lax.dot_general(one, syms[...], NT, preferred_element_type=F32)
    sym_ref[:, :128] = sym[:, :128].astype(BF16)
    sym_ref[:, 128:256] = sym[:, MAIN:MAIN + 128].astype(BF16)
    tail = jnp.where(lane[:16] < 64, sym[:, 128:MAIN], pltpu.roll(sym[:, MAIN + 128:], 64, 1))
    sym_ref[:, 256:] = tail.astype(BF16)


def place_kernel(meta_ref, a_ref, b_ref, c_ref, d_ref, sym_ref, order_ref, out_ref, total, wide, sems):
    meta = [[meta_ref[group, i] for i in range(3)] for group in range(8)]
    for i in range(3):
        rows = slice(i * HEIGHT, (i + 1) * HEIGHT)
        value = a_ref[rows, :].astype(F32) + b_ref[rows, :].astype(F32) + c_ref[rows, :].astype(F32)
        total[:, i * 128:(i + 1) * 128] = (value + d_ref[rows, :].astype(F32)).astype(BF16)
    row = lax.broadcasted_iota(I32, (16, 128), 0)
    copies = []
    for i in range(3):
        lanes = slice(i * 128, (i + 1) * 128)
        sym = jnp.dot(sym_ref[...], order_ref[:, lanes], preferred_element_type=F32).astype(BF16)
        value = jnp.dot(total[...], order_ref[:, lanes], preferred_element_type=F32).astype(BF16)
        for first, start, code in meta:
            start = pl.multiple_of(start, 16)
            mask = sym == code.astype(F32).astype(BF16)
            kept = jnp.where(jnp.concatenate([mask] * (HEIGHT // 16), axis=0), value, jnp.zeros((), BF16))
            head = wide[pl.ds(start, 16), lanes].astype(F32)
            wide[pl.ds(start, 16), lanes] = jnp.where(row < first - start, head, kept[:16].astype(F32)).astype(BF16)
            wide[pl.ds(start + 16, HEIGHT - 16), lanes] = kept[16:]
            wide[pl.ds(start + HEIGHT, 16), lanes] = kept[:16]
        copies.append(pltpu.make_async_copy(wide.at[pl.ds(0, VIRT), lanes], out_ref.at[:, lanes], sems.at[i]))
        copies[i].start()
    for copy in copies:
        copy.wait()


def shift(value, axis, size, by):
    return lax.ppermute(value, axis, [(i, (i + by) % size) for i in range(size)])


def call(kernel, specs, out, scratch=(), out_specs=None, flops=0, moved=0, limit=40):
    return pl.pallas_call(
        kernel,
        in_specs=specs,
        out_specs=out_specs or jax.tree.map(lambda _: VMEM, out),
        out_shape=out,
        scratch_shapes=list(scratch),
        compiler_params=pltpu.CompilerParams(vmem_limit_bytes=limit * 2**20),
        cost_estimate=pl.CostEstimate(flops=flops, bytes_accessed=moved, transcendentals=0),
    )


def shards(virt_sizes, occ_sizes, pair_ids, amplitudes, integrals):
    shape = jax.ShapeDtypeStruct
    packed = call(
        pack_kernel, [HBM] * 4, shape((SLOT, 128), BF16),
        [pltpu.SMEM((8,), I32), pltpu.SMEM((8,), I32), pltpu.SMEM((PAIRS,), I32), pltpu.VMEM((ROWS, VIRT), BF16),
         pltpu.VMEM((ROWS, 1536 + SPAN + 128), F32), pltpu.SemaphoreType.DMA((4,))],
        moved=300000, limit=64,
    )(virt_sizes, occ_sizes, pair_ids, amplitudes)
    mine = lax.all_to_all(packed, "z", 0, 0, tiled=True)
    across = [shift(mine, "x", NX, k) for k in (2, 1, 3)]
    blocks, order, meta, mine = call(
        blocks_kernel, [VMEM, HBM],
        (shape((HEIGHT, DEPTH), BF16), shape((PORTION, PORTION), BF16), shape((8, 128), I32),
         shape((SLOT, 128), BF16)),
        [pltpu.VMEM((8, 2 * WINDOW, VIRT), BF16), pltpu.VMEM((WINDOW, SPAN), BF16),
         pltpu.VMEM((16, 128), I32), pltpu.SemaphoreType.DMA((8,))], moved=16000000, limit=48,
    )(mine, integrals)
    own = jnp.concatenate([mine, across[1], across[0], across[2]], axis=0)
    other = shift(own, "c", NC, 1)
    tile, part = shape((MESSAGE, 128), BF16), shape((2 * HEIGHT, 128), BF16)

    def scratch(columns):
        return [pltpu.VMEM((columns, DEPTH), BF16), pltpu.VMEM((columns, 128), BF16), pltpu.VMEM((HEIGHT, columns), F32)]

    def cost(columns):
        return dict(flops=2 * columns * HEIGHT * DEPTH, moved=4000000)

    two, plus, minus = call(
        functools.partial(own_kernel, (2, 1, 3)), [VMEM] * 2, (part,) * 3, scratch(3 * MAIN), **cost(3 * MAIN)
    )(own, blocks)
    far, terms = [], ()
    for steps, mine in (((2,), (two,)), ((1, 3), (plus, minus))):
        columns = len(steps) * MAIN
        operands = (other, blocks, *terms, *mine)
        terms = call(
            functools.partial(other_kernel, steps, len(terms)), [VMEM] * len(operands), (tile,) * len(steps),
            scratch(columns), **cost(columns)
        )(*operands)
        far += [shift(term, "y", NY, r) for r, term in zip(steps, terms)]
    stay, sym = call(
        stay_kernel, [VMEM] * 3, (tile, shape((16, PORTION), BF16)), scratch(2 * MAIN), flops=20*10**9
    )(own, other, blocks)
    out = call(
        place_kernel, [VMEM] * 7, shape((VIRT, PORTION), BF16),
        [pltpu.VMEM((HEIGHT, PORTION), BF16), pltpu.VMEM((VIRT + WINDOW, PORTION), BF16), pltpu.SemaphoreType.DMA((3,))],
        HBM, moved=2600000,
    )(meta, stay, *far, sym, order)
    return out.T


def solution(mesh):
    grid = Mesh(mesh.devices.reshape(NX, NZ, NC, NY), ("x", "z", "c", "y"))
    vp = ("x", "z", "c")
    in_specs = (P(), P(), P(), P(vp, "y"), P(vp, "y"))
    return jax.shard_map(shards, mesh=grid, in_specs=in_specs, out_specs=P("y", vp), check_vma=False)
```
